32 devices in a mesh: dp: 8 (over y, x, core), tensor: 4 (over z).
Axes of the slice: x: 2, y: 2, z: 4, core: 2. Of those that a mesh axis runs over, the one named last changes fastest.
Arguments:
- tokens: bfloat16 [8192, 3072], P('dp', 'tensor'), may hold values from -6 to 6
- cotangent: bfloat16 [8192, 3072], P('dp', 'tensor'), may hold values from -24 to 24
- codes: int32 [8192, 12288], P('dp', 'tensor'), may hold values from -127 to 127
- row_scale: float32 [8192], P('dp'), may hold values from 0.004 to 0.04
- probe: bfloat16 [3072, 12288], P('dp', 'tensor'), may hold values from -6 to 6
- down_weight: bfloat16 [12288, 3072], P(('tensor', 'dp')), may hold values from -0.0546875 to 0.0546875
Outputs:
- diag_estimate: float32 [3072, 12288], P('dp', 'tensor')
The draws below stay inside these ranges and needn't reach their ends.
All inputs are finite; a program needn't handle non-finite values.
Results may differ from the reference program's by a relative error of at most 0.003.
Values may be sent and summed in bfloat16 or wider, within the bound.
No kernel may reach another device: no remote copies, remote signals or barrier semaphores. Data moves between devices by JAX's collectives and lax.ppermute only.
A program may use at most 192 MiB of HBM per device.

```python
import math
import jax
import jax.numpy as jnp

D = 3072
FF = 12288
TOKENS = 8192


def plant(array, own_key, low, high):
    shape = array.shape
    index_at = [jax.random.randint(jax.random.fold_in(own_key, axis), (), 0, shape[axis]) for axis in range(len(shape))]
    array = array.at[tuple(index_at)].set(low)
    longest = shape.index(max(shape))
    index_at[longest] = (index_at[longest] + 1) % shape[longest]
    return array.at[tuple(index_at)].set(high)


def strengthened(result, own_key, source, target, blocks, factor):
    def block_of(dim):
        return (jnp.arange(result.shape[dim]) // (result.shape[dim] // blocks)).reshape((-1,) + (1,) * (result.ndim - 1 - dim))

    near = jax.random.permutation(own_key, blocks)[block_of(target)]
    far = (block_of(target) + blocks // 2) % blocks
    return jnp.where((block_of(source) == near) | (block_of(source) == far), factor * result, result)


def level_of(rng, shape, shards, smallest, high):
    loudness = 1.0
    for axis_at, blocks in shards:
        draws = jax.random.uniform(jax.random.fold_in(jax.random.fold_in(rng, 6), axis_at), (blocks,), jnp.float32, smallest / len(shards), high / len(shards))
        loudness = loudness * jnp.repeat(jnp.exp(draws), shape[axis_at] // blocks).reshape((-1,) + (1,) * (len(shape) - 1 - axis_at))
    return loudness


def gaussian(key, extent, spread, bound, shards=(), kind=jnp.bfloat16):
    drawn = spread * jax.random.normal(key, extent, jnp.float32)
    if shards:
        drawn = drawn * level_of(key, extent, shards, -0.22, 0.18)
    return jnp.clip(drawn, -bound, bound).astype(kind)


def bell_draw_with(rng, shape, width, reach, split, heavy, held_as=jnp.bfloat16):
    entries = width * jax.random.normal(rng, shape, jnp.float32)
    if split:
        entries = entries * level_of(rng, shape, split, -0.22, 0.18)
    return jnp.clip(strengthened(entries, jax.random.fold_in(rng, 3), *heavy), -reach, reach).astype(held_as)


def setup_inputs(seed: int = 0) -> dict:
    splits = jax.random.split(jax.random.key(seed), 7)
    return {
        "tokens": bell_draw_with(splits[0], (TOKENS, D), 1.0, 6.0, ((0, 8), (1, 4)), (0, 1, 8, 2.0)),
        "cotangent": gaussian(splits[1], (TOKENS, D), 4.0, 24.0, ((0, 8), (1, 4))),
        "codes": plant(jax.random.randint(splits[2], (TOKENS, FF), -127, 128), jax.random.fold_in(splits[2], 1), -127, 127).astype(jnp.int32),
        "row_scale": jnp.clip(jnp.exp(math.log(0.04) - 2.30258502 * jax.random.uniform(splits[3], (TOKENS,), jnp.float32) ** level_of(splits[3], (TOKENS,), ((0, 8),), -0.2, 0.2)), 0.004, 0.04),
        "probe": gaussian(splits[4], (D, FF), 1.0, 6.0, ((0, 8), (1, 4))),
        "down_weight": gaussian(splits[5], (FF, D), FF ** -0.5, 0.0546875, ((0, 32),)),
    }


def reference(tokens, cotangent, codes, row_scale, probe, down_weight):
    active = codes.astype(jnp.float32) * row_scale[:, None]
    density = jnp.exp(-0.5 * active * active) * (1.0 / math.sqrt(2.0 * math.pi))
    curvature = density * (2.0 - active * active)
    tangent = jnp.dot(tokens, probe, preferred_element_type=jnp.float32)
    backward = jnp.dot(cotangent, down_weight.T, preferred_element_type=jnp.float32)
    mixed_term = (backward * curvature * tangent).astype(jnp.bfloat16)
    hessian = jnp.dot(tokens.T, mixed_term, preferred_element_type=jnp.float32)
    return probe.astype(jnp.float32) * hessian * (1.0 / TOKENS)
```

```python
import math

import jax
import jax.numpy as jnp
from jax import lax
from jax.sharding import PartitionSpec as P

inv_root = 1.0 / math.sqrt(2.0 * math.pi)
chunks = 4
f32 = jnp.float32
bf16 = jnp.bfloat16


def folded(n):
    return [0] + list(range(1, n, 2)) + list(range(n - 2 + n % 2, 0, -2)) if n > 1 else [0]


def shift(n, stride, total, by):
    pairs = []
    for i in range(total):
        digit = (i // stride) % n
        pairs.append((i, i + (((digit + by) % n) - digit) * stride))
    return pairs


def ring_gather(block, order, starts):
    n = len(order)
    pairs = [(order[i], order[(i + 1) % n]) for i in range(n)]
    full = jnp.zeros((block.shape[0], block.shape[1] * n), block.dtype)
    held = block
    full = lax.dynamic_update_slice(full, held, (0, starts[0]))
    for step in range(1, n):
        held = lax.ppermute(held, "tensor", pairs)
        full = lax.dynamic_update_slice(full, held, (0, starts[step]))
    return full


def reduce_over(parts, dim, n, stride, total, digit):
    own = lax.dynamic_index_in_dim(parts, digit, dim, keepdims=True)
    for by in range(1, n):
        send = lax.dynamic_index_in_dim(parts, lax.rem(digit + by, n), dim, keepdims=True).astype(bf16)
        own = own + lax.ppermute(send, "dp", shift(n, stride, total, by)).astype(f32)
    return own


def shards(tokens, cotangent, codes, row_scale, probe, down_weight):
    dp, tp = lax.axis_size("dp"), lax.axis_size("tensor")
    cores, xs = 2, 2
    ys = dp // (cores * xs)
    me = lax.axis_index("dp")
    core, x, y = lax.rem(me, cores), lax.rem(lax.div(me, cores), xs), lax.div(me, cores * xs)
    tok_rows = tokens.shape[0]
    rows, hidden = probe.shape
    order = folded(tp)
    width = tokens.shape[1]
    table = [[width * order[(order.index(i) - s) % tp] for s in range(tp)] for i in range(tp)]
    starts = lax.dynamic_index_in_dim(
        jnp.array(table, jnp.int32), lax.axis_index("tensor"), 0, keepdims=False
    )
    wide = hidden // chunks

    cot_full = ring_gather(cotangent, order, starts)
    tok_full = ring_gather(tokens, order, starts)
    down_full = lax.all_gather(down_weight, "dp", axis=0, tiled=True)
    active = codes.astype(f32) * row_scale[:, None]
    curvature = jnp.exp(-0.5 * active * active) * inv_root * (2.0 - active * active)
    backward = lax.dot_general(
        cot_full, down_full, (((1,), (1,)), ((), ())), preferred_element_type=f32
    )
    bent = backward * curvature

    by_core = tok_full.reshape(tok_rows, ys * xs, cores, rows)
    mine = lax.dynamic_index_in_dim(by_core, core, 2, keepdims=False).reshape(tok_rows, -1)
    other = lax.dynamic_index_in_dim(by_core, 1 - core, 2, keepdims=False).reshape(tok_rows, -1)

    pieces = []
    for j in range(chunks):
        cut = slice(j * wide, (j + 1) * wide)
        probe_full = lax.all_gather(probe[:, cut], "dp", axis=0, tiled=True)
        tangent = jnp.dot(tok_full, probe_full, preferred_element_type=f32)
        mixed = (bent[:, cut] * tangent).astype(bf16)
        away = lax.dot_general(other, mixed, (((0,), (0,)), ((), ())), preferred_element_type=f32)
        came = lax.ppermute(away.astype(bf16), "dp", shift(cores, 1, dp, 1))
        kept = lax.dot_general(mine, mixed, (((0,), (0,)), ((), ())), preferred_element_type=f32)
        chip = (kept + came.astype(f32)).reshape(ys, xs, rows, wide)
        half = wide // 2
        first, second = chip[..., :half], chip[..., half:]
        first = reduce_over(first, 1, xs, cores, dp, x)
        first = reduce_over(first, 0, ys, cores * xs, dp, y)
        second = reduce_over(second, 0, ys, cores * xs, dp, y)
        second = reduce_over(second, 1, xs, cores, dp, x)
        pieces += [first.reshape(rows, half), second.reshape(rows, half)]
    hessian = jnp.concatenate(pieces, axis=1)
    return probe.astype(f32) * hessian * (1.0 / (tok_rows * dp))


def solution(mesh):
    placed = (
        P("dp", "tensor"),
        P("dp", "tensor"),
        P("dp", "tensor"),
        P("dp"),
        P("dp", "tensor"),
        P(("tensor", "dp"), None),
    )
    return jax.shard_map(
        shards, mesh=mesh, in_specs=placed, out_specs=P("dp", "tensor"), check_vma=False
    )
```

```python
import functools
import math

import jax
import jax.numpy as jnp
from jax import lax
from jax.experimental import pallas as pl
from jax.experimental.pallas import tpu as pltpu
from jax.sharding import PartitionSpec as P

inv_root = 1.0 / math.sqrt(2.0 * math.pi)
sixths = (1, 2, 2, 1)
f32 = jnp.float32
bf16 = jnp.bfloat16
vmem = 56 * 1024 * 1024


def folded(n):
    return [0] + list(range(1, n, 2)) + list(range(n - 2 + n % 2, 0, -2)) if n > 1 else [0]


def shift(n, stride, total, by):
    pairs = []
    for i in range(total):
        digit = (i // stride) % n
        pairs.append((i, i + (((digit + by) % n) - digit) * stride))
    return pairs


def params():
    return pltpu.CompilerParams(vmem_limit_bytes=vmem)


def cost(flops, nbytes):
    return pl.CostEstimate(flops=int(flops), bytes_accessed=int(nbytes), transcendentals=0)


def place_body(count, by_column, width, at, *refs):
    pieces, out, sems = refs[:count], refs[-2], refs[-1]
    copies = []
    for i in range(count):
        if by_column:
            where = out.at[:, pl.ds(pl.multiple_of(at[i] * width, 128), width)]
        else:
            where = out.at[at[i]]
        copies.append(pltpu.make_async_copy(pieces[i], where, sems.at[i]))
    for c in copies:
        c.start()
    for c in copies:
        c.wait()


def place_rows(pieces, at, slots):
    shape = pieces[0].shape
    count = len(pieces)
    total = slots * shape[0] * shape[1] * 2
    out = pl.pallas_call(
        functools.partial(place_body, count, False, shape[0]),
        grid_spec=pltpu.PrefetchScalarGridSpec(
            num_scalar_prefetch=1,
            grid=(1,),
            in_specs=[pl.BlockSpec(memory_space=pl.ANY)] * count,
            out_specs=pl.BlockSpec(memory_space=pl.ANY),
            scratch_shapes=[pltpu.SemaphoreType.DMA((count,))],
        ),
        out_shape=jax.ShapeDtypeStruct((slots,) + shape, pieces[0].dtype),
        compiler_params=params(),
        cost_estimate=cost(0, 2 * total),
        name="place_rows",
    )(at, *pieces)
    return out.reshape(slots * shape[0], shape[1])


def split_body(count, half, core, aliased, at, *refs):
    pieces = refs[:count]
    mine, other, sems = refs[-3], refs[-2], refs[-1]
    own = core[0]
    copies = []
    for i in range(count):
        into = pl.ds(pl.multiple_of(at[i] * half, 128), half)
        for k, (out, which) in enumerate(((mine, own), (other, 1 - own))):
            source = pieces[i].at[:, pl.ds(pl.multiple_of(which * half, 128), half)]
            copies.append(pltpu.make_async_copy(source, out.at[:, into], sems.at[2 * i + k]))
    for c in copies:
        c.start()
    for c in copies:
        c.wait()


def split_cores(pieces, at, core, slots, before=None):
    count = len(pieces)
    tok, wide = pieces[0].shape
    half = wide // 2
    shape = jax.ShapeDtypeStruct((tok, slots * half), pieces[0].dtype)

    def body(core_ref, at_ref, *refs):
        split_body(count, half, core_ref, before, at_ref, *refs)

    extra = list(before) if before else []
    return pl.pallas_call(
        body,
        grid_spec=pltpu.PrefetchScalarGridSpec(
            num_scalar_prefetch=2,
            grid=(1,),
            in_specs=[pl.BlockSpec(memory_space=pl.ANY)] * (count + len(extra)),
            out_specs=[pl.BlockSpec(memory_space=pl.ANY)] * 2,
            scratch_shapes=[pltpu.SemaphoreType.DMA((2 * count,))],
        ),
        out_shape=[shape, shape],
        input_output_aliases={2 + count: 0, 3 + count: 1} if extra else {},
        compiler_params=params(),
        cost_estimate=cost(0, 4 * count * tok * wide),
        name="split_cores",
    )(core.reshape(1), at, *pieces, *extra)


def split_plain(pieces, at, core):
    tok, wide = pieces[0].shape
    full = jnp.zeros((tok, wide * len(pieces)), pieces[0].dtype)
    for i, piece in enumerate(pieces):
        full = lax.dynamic_update_slice(full, piece, (0, at[i] * wide))
    full = full.reshape(tok, len(pieces), 2, wide // 2)
    return [
        lax.dynamic_index_in_dim(full, which, 2, keepdims=False).reshape(tok, -1)
        for which in (core, 1 - core)
    ]


def whole(shape):
    return pl.BlockSpec(shape, lambda *_: (0,) * len(shape))


def bent_body(count, width, at, scale, codes, down, *refs):
    shards, out = refs[:count], refs[count]
    total = None
    for s in range(count):
        cols = pl.ds(pl.multiple_of(at[s] * width, 128), width)
        term = lax.dot_general(
            shards[s][...], down[:, cols], (((1,), (1,)), ((), ())), preferred_element_type=f32
        )
        total = term if total is None else total + term
    active = codes[...].astype(f32) * scale[...]
    square = active * active
    out[...] = total * (jnp.exp(-0.5 * square) * inv_root * (2.0 - square))


def bent_of(shards, at, row_scale, codes, down_full):
    count = len(shards)
    tok, width = shards[0].shape
    hidden, feats = down_full.shape
    tile = 512
    return pl.pallas_call(
        functools.partial(bent_body, count, width),
        grid_spec=pltpu.PrefetchScalarGridSpec(
            num_scalar_prefetch=1,
            grid=(hidden // tile,),
            in_specs=[
                whole((tok, 1)),
                pl.BlockSpec((tok, tile), lambda j, at: (0, j)),
                pl.BlockSpec((tile, feats), lambda j, at: (j, 0)),
            ]
            + [whole((tok, width))] * count,
            out_specs=pl.BlockSpec((tok, tile), lambda j, at: (0, j)),
        ),
        out_shape=jax.ShapeDtypeStruct((tok, hidden), f32),
        compiler_params=params(),
        cost_estimate=cost(2 * tok * feats * hidden, hidden * (2 * feats + 8 * tok)),
        name="bent",
    )(at, row_scale[:, None], codes, down_full, *shards)


def partial_body(count, width, at, probe, *refs):
    shards, out = refs[:count], refs[count]
    total = None
    for s in range(count):
        rows = pl.ds(pl.multiple_of(at[s] * width, 128), width)
        term = jnp.dot(shards[s][...], probe[rows, :], preferred_element_type=f32)
        total = term if total is None else total + term
    out[...] = total


def partial_tangent(shards, at, probe_full):
    count = len(shards)
    tok, width = shards[0].shape
    feats, hidden = probe_full.shape
    tile = 512
    return pl.pallas_call(
        functools.partial(partial_body, count, width),
        grid_spec=pltpu.PrefetchScalarGridSpec(
            num_scalar_prefetch=1,
            grid=(hidden // tile,),
            in_specs=[pl.BlockSpec((feats, tile), lambda j, at: (0, j))]
            + [whole((tok, width))] * count,
            out_specs=pl.BlockSpec((tok, tile), lambda j, at: (0, j)),
        ),
        out_shape=jax.ShapeDtypeStruct((tok, hidden), f32),
        compiler_params=params(),
        cost_estimate=cost(2 * tok * count * width * hidden, hidden * (2 * feats + 4 * tok)),
        name="partial_tangent",
    )(at, probe_full, *shards)


def mixed_body(at, shard, probe, begun, bent, out):
    tangent = begun[...] + jnp.dot(shard[...], probe[...], preferred_element_type=f32)
    out[...] = (bent[...] * tangent).astype(bf16)


def mixed_of(shard, at, probe_full, begun, bent, first, wide):
    tok, width = shard.shape
    tile = wide // 2
    base = first // tile
    last = at.shape[0] - 1
    return pl.pallas_call(
        mixed_body,
        grid_spec=pltpu.PrefetchScalarGridSpec(
            num_scalar_prefetch=1,
            grid=(2,),
            in_specs=[
                whole((tok, width)),
                pl.BlockSpec((width, tile), lambda j, at: (at[last], base + j)),
                pl.BlockSpec((tok, tile), lambda j, at: (0, base + j)),
                pl.BlockSpec((tok, tile), lambda j, at: (0, base + j)),
            ],
            out_specs=pl.BlockSpec((tok, tile), lambda j, at: (0, j)),
        ),
        out_shape=jax.ShapeDtypeStruct((tok, wide), bf16),
        compiler_params=params(),
        cost_estimate=cost(2 * tok * width * wide, wide * (2 * width + 10 * tok)),
        name="mixed",
    )(at, shard, probe_full, begun, bent)


def ring_gather(block, order):
    n = len(order)
    pairs = [(order[i], order[(i + 1) % n]) for i in range(n)]
    held = [block]
    for _ in range(1, n):
        held.append(lax.ppermute(held[-1], "tensor", pairs))
    return held


def plane_gather(block, cores, xs, ys, core, x, y):
    dp = cores * xs * ys
    rows = block.shape[0] // 2

    def chip(a, by):
        return lax.ppermute(a, "dp", shift(xs, cores, dp, by))

    def up(a, by):
        return lax.ppermute(a, "dp", shift(ys, cores * xs, dp, by))

    top, low = block[:rows], block[rows:]
    held = [(top, 0, 0, 0), (low, 1, 0, 0)]
    for i in range(1, xs):
        across = chip(top, i)
        held += [(across, 0, i, 0), (chip(low, i), 1, i, 0)]
        held += [(up(across, k), 0, i, k) for k in range(1, ys)]
    for k in range(1, ys):
        above = up(low, k)
        held += [(above, 1, 0, k), (up(top, k), 0, 0, k)]
        held += [(chip(above, i), 1, i, k) for i in range(1, xs)]
    pieces, at = [], []
    for by in range(cores):
        for piece, half, i, k in held:
            pieces.append(lax.ppermute(piece, "dp", shift(cores, 1, dp, by)) if by else piece)
            there = (lax.rem(y + ys - k, ys) * xs + lax.rem(x + xs - i, xs)) * cores
            at.append((there + lax.rem(core + cores - by, cores)) * 2 + half)
    return place_rows(pieces, jnp.stack(at), 2 * dp)


def reduce_over(parts, dim, n, stride, total, digit):
    own = lax.dynamic_index_in_dim(parts, digit, dim, keepdims=True)
    for by in range(1, n):
        send = lax.dynamic_index_in_dim(parts, lax.rem(digit + by, n), dim, keepdims=True)
        own = own + lax.ppermute(send.astype(bf16), "dp", shift(n, stride, total, by)).astype(f32)
    return own


def shards(tokens, cotangent, codes, row_scale, probe, down_weight):
    dp, tp = lax.axis_size("dp"), lax.axis_size("tensor")
    cores, xs = 2, 2
    ys = dp // (cores * xs)
    me = lax.axis_index("dp")
    core, x, y = lax.rem(me, cores), lax.rem(lax.div(me, cores), xs), lax.div(me, cores * xs)
    tok_rows = tokens.shape[0]
    rows, hidden = probe.shape
    order = folded(tp)
    table = [[order[(order.index(i) - s) % tp] for s in range(tp)] for i in range(tp)]
    at = lax.dynamic_index_in_dim(
        jnp.array(table, jnp.int32), lax.axis_index("tensor"), 0, keepdims=False
    )

    cot = ring_gather(cotangent, order)
    tok = ring_gather(tokens, order)
    down_full = lax.all_gather(down_weight, "dp", axis=0, tiled=True)
    probe_full = plane_gather(probe, cores, xs, ys, core, x, y)

    bent = bent_of(cot, at, row_scale, codes, down_full)
    begun = partial_tangent(tok[:-1], at, probe_full)
    if rows % 128:
        mine, other = split_plain(tok, at, core)
    else:
        early = split_cores(tok[:-1], at[:-1], core, tp)
        mine, other = split_cores(tok[-1:], at[-1:], core, tp, early)

    pieces = []
    first = 0
    for part in sixths:
        wide = hidden * part // sum(sixths)
        mixed = mixed_of(tok[-1], at, probe_full, begun, bent, first, wide)
        first += wide
        away = lax.dot_general(other, mixed, (((0,), (0,)), ((), ())), preferred_element_type=f32)
        came = lax.ppermute(away.astype(bf16), "dp", shift(cores, 1, dp, 1))
        kept = lax.dot_general(mine, mixed, (((0,), (0,)), ((), ())), preferred_element_type=f32)
        both = (kept + came.astype(f32)).reshape(ys, xs, rows, wide)
        half = wide // 2
        left, right = both[..., :half], both[..., half:]
        left = reduce_over(left, 1, xs, cores, dp, x)
        left = reduce_over(left, 0, ys, cores * xs, dp, y)
        right = reduce_over(right, 0, ys, cores * xs, dp, y)
        right = reduce_over(right, 1, xs, cores, dp, x)
        pieces += [left.reshape(rows, half), right.reshape(rows, half)]
    hessian = jnp.concatenate(pieces, axis=1)
    return probe.astype(f32) * hessian * (1.0 / (tok_rows * dp))


def solution(mesh):
    placed = (
        P("dp", "tensor"),
        P("dp", "tensor"),
        P("dp", "tensor"),
        P("dp"),
        P("dp", "tensor"),
        P(("tensor", "dp"), None),
    )
    return jax.shard_map(
        shards, mesh=mesh, in_specs=placed, out_specs=P("dp", "tensor"), check_vma=False
    )
```

```python
import functools
import math

import jax
import jax.numpy as jnp
from jax import lax
from jax.experimental import pallas as pl
from jax.experimental.pallas import tpu as pltpu
from jax.sharding import PartitionSpec as P

inv_root = 1.0 / math.sqrt(2.0 * math.pi)
sixths = (1, 2, 2, 1)
f32 = jnp.float32
bf16 = jnp.bfloat16
vmem = 56 * 1024 * 1024


def folded(n):
    return [0] + list(range(1, n, 2)) + list(range(n - 2 + n % 2, 0, -2)) if n > 1 else [0]


def shift(n, stride, total, by):
    pairs = []
    for i in range(total):
        digit = (i // stride) % n
        pairs.append((i, i + (((digit + by) % n) - digit) * stride))
    return pairs


light = pl.CostEstimate(flops=0, bytes_accessed=1024, transcendentals=0)


def params():
    return pltpu.CompilerParams(vmem_limit_bytes=vmem)


def split_body(count, half, core, at, *refs):
    pieces = refs[:count]
    outs, held, sems = refs[-4:-2], refs[-2], refs[-1]
    copies = []
    for i in range(count):
        rows = pl.ds(pl.multiple_of(at[i] * half, half), half)
        for k, which in enumerate((core[0], 1 - core[0])):
            slot = 2 * i + k
            cols = pl.ds(pl.multiple_of(which * half, 128), half)
            held[slot] = pieces[i][:, cols].T
            copies.append(pltpu.make_async_copy(held.at[slot], outs[k].at[rows], sems.at[slot]))
            copies[-1].start()
    for c in copies:
        c.wait()


def split_cores(pieces, at, core, slots, before=()):
    count = len(pieces)
    tok, wide = pieces[0].shape
    half = wide // 2
    shape = jax.ShapeDtypeStruct((slots * half, tok), bf16)
    return pl.pallas_call(
        functools.partial(split_body, count, half),
        grid_spec=pltpu.PrefetchScalarGridSpec(
            num_scalar_prefetch=2,
            grid=(1,),
            in_specs=[whole((tok, wide))] * count
            + [pl.BlockSpec(memory_space=pl.ANY)] * len(before),
            out_specs=[pl.BlockSpec(memory_space=pl.ANY)] * 2,
            scratch_shapes=[
                pltpu.VMEM((2 * count, half, tok), bf16),
                pltpu.SemaphoreType.DMA((2 * count,)),
            ],
        ),
        out_shape=[shape, shape],
        input_output_aliases={2 + count: 0, 3 + count: 1} if before else {},
        compiler_params=params(),
        cost_estimate=light,
        name="split_cores",
    )(core.reshape(1), at, *pieces, *before)


def split_plain(pieces, at, core):
    tok, wide = pieces[0].shape
    full = jnp.zeros((tok, wide * len(pieces)), pieces[0].dtype)
    for i, piece in enumerate(pieces):
        full = lax.dynamic_update_slice(full, piece, (0, at[i] * wide))
    full = full.reshape(tok, len(pieces), 2, wide // 2)
    return [
        lax.dynamic_index_in_dim(full, which, 2, keepdims=False).reshape(tok, -1).T
        for which in (core, 1 - core)
    ]


def whole(shape):
    return pl.BlockSpec(shape, lambda *_: (0,) * len(shape))


def bent_body(count, parts, width, at, scale, codes, down, *refs):
    shards, out = refs[: count * parts], refs[count * parts]
    for h in range(parts):
        tall = shards[h].shape[0]
        total = None
        for s in range(count):
            cols = pl.ds(pl.multiple_of(at[s] * width, 128), width)
            term = lax.dot_general(
                shards[s * parts + h][...],
                down[:, cols],
                (((1,), (1,)), ((), ())),
                preferred_element_type=f32,
            )
            total = term if total is None else total + term
        rows = pl.ds(h * tall, tall)
        active = codes[rows, :].astype(f32) * scale[rows, :]
        square = active * active
        out[rows, :] = total * (jnp.exp(-0.5 * square) * inv_root * (2.0 - square))


def bent_of(shards, at, row_scale, codes, down_full, first, wide):
    count, parts = len(shards), len(shards[0])
    tall, width = shards[0][0].shape
    tok = tall * parts
    feats = down_full.shape[1]
    tile = math.gcd(wide, math.gcd(first, 512))
    base = first // tile
    return pl.pallas_call(
        functools.partial(bent_body, count, parts, width),
        grid_spec=pltpu.PrefetchScalarGridSpec(
            num_scalar_prefetch=1,
            grid=(wide // tile,),
            in_specs=[
                whole((tok, 1)),
                pl.BlockSpec((tok, tile), lambda j, at: (0, base + j)),
                pl.BlockSpec((tile, feats), lambda j, at: (base + j, 0)),
            ]
            + [whole((tall, width))] * (count * parts),
            out_specs=pl.BlockSpec((tok, tile), lambda j, at: (0, j)),
        ),
        out_shape=jax.ShapeDtypeStruct((tok, wide), f32),
        compiler_params=params(),
        cost_estimate=light,
        name="bent",
    )(at, row_scale[:, None], codes, down_full, *[p for piece in shards for p in piece])


def partial_body(count, parts, width, spots, plan, arrays, tile, at, slots, *refs):
    pieces, refs = refs[:arrays], refs[arrays:]
    shards = refs[: count * parts]
    out, last, held, sems = refs[count * parts :]
    step = pl.program_id(0)

    @pl.when(step == 0)
    def _():
        copies = []
        for i, (which, first, size) in enumerate(plan):
            into = held.at[pl.ds(pl.multiple_of(slots[i] * spots, spots), size)]
            source = pieces[which].at[pl.ds(first, size)]
            copies.append(pltpu.make_async_copy(source, into, sems.at[i]))
        for c in copies:
            c.start()
        for c in copies:
            c.wait()

    cols = pl.ds(pl.multiple_of(step * tile, tile), tile)
    for h in range(parts):
        tall = shards[h].shape[0]
        total = None
        for s in range(count):
            rows = pl.ds(pl.multiple_of(at[s] * width, width), width)
            term = jnp.dot(
                shards[s * parts + h][...], held[rows, cols], preferred_element_type=f32
            )
            total = term if total is None else total + term
        out[pl.ds(h * tall, tall), :] = total
    last[...] = held[pl.ds(pl.multiple_of(at[count] * width, width), width), cols]


def partial_tangent(shards, at, pieces, slots, spots, feats):
    count, parts = len(shards), len(shards[0])
    tall, width = shards[0][0].shape
    tok = tall * parts
    hidden = pieces[0][0].shape[1]
    tile = 512
    arrays, plan = [], []
    for piece, first, size in pieces:
        which = [i for i, a in enumerate(arrays) if a is piece]
        if not which:
            arrays.append(piece)
        plan.append((which[0] if which else len(arrays) - 1, first, size))
    return pl.pallas_call(
        functools.partial(
            partial_body, count, parts, width, spots, plan, len(arrays), tile
        ),
        grid_spec=pltpu.PrefetchScalarGridSpec(
            num_scalar_prefetch=2,
            grid=(hidden // tile,),
            in_specs=[pl.BlockSpec(memory_space=pl.ANY)] * len(arrays)
            + [whole((tall, width))] * (count * parts),
            out_specs=[
                pl.BlockSpec((tok, tile), lambda j, *_: (0, j)),
                pl.BlockSpec((width, tile), lambda j, *_: (0, j)),
            ],
            scratch_shapes=[
                pltpu.VMEM((feats, hidden), bf16),
                pltpu.SemaphoreType.DMA((len(pieces),)),
            ],
        ),
        out_shape=[
            jax.ShapeDtypeStruct((tok, hidden), f32),
            jax.ShapeDtypeStruct((width, hidden), bf16),
        ],
        compiler_params=params(),
        cost_estimate=light,
        name="partial_tangent",
    )(at, slots, *arrays, *[p for piece in shards for p in piece])


def front_body(shard, probe, begun, bent, other, mixed, away):
    tangent = begun[...] + jnp.dot(shard[...], probe[...], preferred_element_type=f32)
    mixed[...] = (bent[...] * tangent).astype(bf16)
    away[...] = jnp.dot(other[...], mixed[...], preferred_element_type=f32).astype(bf16)


def front_of(shard, last, begun, bent, other, first):
    tok, width = shard.shape
    wide = bent.shape[1]
    half = other.shape[0]
    tile = math.gcd(wide, math.gcd(first, 256))
    base = first // tile
    return pl.pallas_call(
        front_body,
        grid=(wide // tile,),
        in_specs=[
            whole((tok, width)),
            pl.BlockSpec((width, tile), lambda j: (0, base + j)),
            pl.BlockSpec((tok, tile), lambda j: (0, base + j)),
            pl.BlockSpec((tok, tile), lambda j: (0, j)),
            whole(other.shape),
        ],
        out_specs=[
            pl.BlockSpec((tok, tile), lambda j: (0, j)),
            pl.BlockSpec((half, tile), lambda j: (0, j)),
        ],
        out_shape=[
            jax.ShapeDtypeStruct((tok, wide), bf16),
            jax.ShapeDtypeStruct((half, wide), bf16),
        ],
        compiler_params=params(),
        cost_estimate=light,
        name="front",
    )(shard, last, begun, bent, other)


def back_body(xs, ys, rows, steps, me, mine, mixed, came, keep_x, keep_y, to_x, to_y):
    x, y = me[0], me[1]

    def block(at_y, at_x):
        part = pl.ds(pl.multiple_of((at_y * xs + at_x) * rows, rows), rows)
        total = jnp.dot(mine[part, :], mixed[...], preferred_element_type=f32)
        return total + came[part, :].astype(f32)

    @pl.when(pl.program_id(0) < steps)
    def _():
        for k in range(ys):
            for i in range(1, xs):
                to_x[k, i - 1] = block(k, lax.rem(x + i, xs)).astype(bf16)
            keep_x[k, 0] = block(k, x)

    @pl.when(pl.program_id(0) >= steps)
    def _():
        for i in range(xs):
            for k in range(1, ys):
                to_y[k - 1, i] = block(lax.rem(y + k, ys), i).astype(bf16)
            keep_y[0, i] = block(y, i)


def back_of(mine, mixed, came, x, y, xs, ys, rows):
    tok, wide = mixed.shape
    side = wide // 2
    tile = math.gcd(side, 256)
    steps = side // tile

    def left(j, me):
        return (0, 0, 0, jnp.minimum(j, steps - 1))

    def right(j, me):
        return (0, 0, 0, jnp.maximum(j - steps, 0))

    shapes = [(ys, 1, rows), (1, xs, rows), (ys, xs - 1, rows), (ys - 1, xs, rows)]
    kinds = [f32, f32, bf16, bf16]
    return pl.pallas_call(
        functools.partial(back_body, xs, ys, rows, steps),
        grid_spec=pltpu.PrefetchScalarGridSpec(
            num_scalar_prefetch=1,
            grid=(2 * steps,),
            in_specs=[
                whole(mine.shape),
                pl.BlockSpec((tok, tile), lambda j, me: (0, j)),
                pl.BlockSpec((mine.shape[0], tile), lambda j, me: (0, j)),
            ],
            out_specs=[
                pl.BlockSpec(shape + (tile,), where)
                for shape, where in zip(shapes, (left, right, left, right))
            ],
        ),
        out_shape=[
            jax.ShapeDtypeStruct(shape + (side,), kind) for shape, kind in zip(shapes, kinds)
        ],
        compiler_params=params(),
        cost_estimate=light,
        name="back",
    )(jnp.stack([x, y]), mine, mixed, came)


def after(ready, *values):
    out = lax.optimization_barrier((ready, *values))
    return out[0], (out[1] if len(values) == 1 else list(out[1:]))


def ring_step(block, order):
    n = len(order)
    pairs = [(order[i], order[(i + 1) % n]) for i in range(n)]
    return lax.ppermute(block, "tensor", pairs)


def swapped(block, dp, cores):
    return lax.ppermute(block, "dp", shift(cores, 1, dp, 1))


def parted(parts, dim, n, digit):
    own = lax.dynamic_index_in_dim(parts, digit, dim, keepdims=True)
    sends = [
        lax.dynamic_index_in_dim(parts, lax.rem(digit + by, n), dim, keepdims=True).astype(bf16)
        for by in range(1, n)
    ]
    return own, sends


def sent(sends, n, stride, total):
    return [
        lax.ppermute(send, "dp", shift(n, stride, total, by + 1)) for by, send in enumerate(sends)
    ]


def summed(own, received):
    for r in received:
        own = own + r.astype(f32)
    return own


def shards(tokens, cotangent, codes, row_scale, probe, down_weight):
    dp, tp = lax.axis_size("dp"), lax.axis_size("tensor")
    cores, xs = 2, 2
    ys = dp // (cores * xs)
    me = lax.axis_index("dp")
    core, x, y = lax.rem(me, cores), lax.rem(lax.div(me, cores), xs), lax.div(me, cores * xs)
    tok_rows = tokens.shape[0]
    rows, hidden = probe.shape
    order = folded(tp)
    table = [[order[(order.index(i) - s) % tp] for s in range(tp)] for i in range(tp)]
    at = lax.dynamic_index_in_dim(
        jnp.array(table, jnp.int32), lax.axis_index("tensor"), 0, keepdims=False
    )

    edges = [hidden * sum(sixths[:j]) // sum(sixths) for j in range(len(sixths) + 1)]
    x_way, y_way = (xs, cores), (ys, cores * xs)

    def over(block, way, by):
        return lax.ppermute(block, "dp", shift(way[0], way[1], dp, by))

    cot, tok = [cotangent], [tokens]
    for s in range(1, tp):
        cot.append(ring_step(cot[-1], order))
        tok.append(ring_step(tok[-1], order))
        if s == 1:
            across = [over(probe, x_way, i) for i in range(1, xs)]
            above = [over(probe, y_way, k) for k in range(1, ys)]
            far = []
            for i in range(1, xs):
                for k in range(1, ys):
                    far.append(over(across[i - 1][: rows // 2], y_way, k))
                    far.append(over(above[k - 1][rows // 2 :], x_way, i))
            near = [(p, swapped(p, dp, cores)) for p in (probe, *across, *above)]
        if s < tp - 1:
            cot[s], tok[s] = lax.optimization_barrier((cot[s], tok[s]))
    far = [(p, swapped(p, dp, cores)) for p in far]
    down_full = lax.all_gather(down_weight, "dp", axis=0, tiled=True)

    pieces, slots = [], []

    def hold(pair, half, i, k):
        chip = (lax.rem(y + ys - k, ys) * xs + lax.rem(x + xs - i, xs)) * cores
        for piece, whose in zip(pair, (core, 1 - core)):
            pieces.append((piece, 0, piece.shape[0]))
            slots.append((chip + whose) * 2 + half)

    spots = [(0, 0)] + [(i, 0) for i in range(1, xs)] + [(0, k) for k in range(1, ys)]
    for pair, (i, k) in zip(near, spots):
        hold(pair, 0, i, k)
    spots = [(half, i, k) for i in range(1, xs) for k in range(1, ys) for half in range(2)]
    for pair, spot in zip(far, spots):
        hold(pair, *spot)
    begun, last = partial_tangent(
        [[t] for t in tok[:-1]], at, pieces, jnp.stack(slots), rows // 2, rows * dp
    )
    begun, cot[-1] = after(begun, cot[-1])
    plain = rows % 128 != 0
    if not plain:
        early = list(split_cores(tok[:-1], at[:-1], core, tp))
        early[0], cot[-1] = after(early[0], cot[-1])
    bent = [
        bent_of(
            [[c] for c in cot], at, row_scale, codes, down_full, edges[j], edges[j + 1] - edges[j]
        )
        for j in range(len(sixths))
    ]
    *bent, tok[-1] = lax.optimization_barrier((*bent, tok[-1]))
    if plain:
        mine, other = split_plain(tok, at, core)
    else:
        mine, other = split_cores(tok[-1:], at[-1:], core, tp, early)

    count = len(sixths)
    out = {}

    def finish(j, keeps, arrived):
        middle = (edges[j] + edges[j + 1]) // 2
        for k, (a, b) in enumerate(((edges[j], middle), (middle, edges[j + 1]))):
            hessian = summed(keeps[k], arrived[k]).reshape(rows, b - a)
            out[2 * j + k] = probe[:, a:b].astype(f32) * hessian * (1.0 / (tok_rows * dp))

    def front(j):
        return front_of(tok[-1], last, begun, bent[j], other, edges[j])

    fronts = {0: front(0)}
    came = {0: swapped(fronts[0][1], dp, cores)}
    mixed = fronts[0][0]
    if count > 1:
        mixed, bent[1] = lax.optimization_barrier((mixed, bent[1]))
        following, away = front(1)
        mixed, following, away, came[0] = lax.optimization_barrier(
            (mixed, following, away, came[0])
        )
        came[1] = swapped(away, dp, cores)
    behind = None
    for j in range(count):
        keep_x, keep_y, to_x, to_y = back_of(mine, mixed, came[j], x, y, xs, ys, rows)
        if behind is not None:
            keeps, arrived = behind
            to_x, to_y, arrived = lax.optimization_barrier((to_x, to_y, arrived))
            finish(j - 1, keeps, arrived)
        ahead = j + 2 < count
        if ahead:
            to_x, to_y, bent[j + 2] = lax.optimization_barrier((to_x, to_y, bent[j + 2]))
        from_x = [over(to_x[:, i - 1 : i], x_way, i) for i in range(1, xs)]
        from_y = [over(to_y[k - 1 : k], y_way, k) for k in range(1, ys)]
        if ahead:
            beyond, away = front(j + 2)
            from_x, from_y, away = lax.optimization_barrier((from_x, from_y, away))
            came[j + 2] = swapped(away, dp, cores)
        left, left_sends = parted(summed(keep_x, from_x), 0, ys, y)
        right, right_sends = parted(summed(keep_y, from_y), 1, xs, x)
        if j + 1 < count:
            left_sends, right_sends, mixed = lax.optimization_barrier(
                (left_sends, right_sends, following)
            )
        if ahead:
            following = beyond
        behind = (left, right), (sent(left_sends, *y_way, dp), sent(right_sends, *x_way, dp))
    finish(count - 1, *behind)
    return jnp.concatenate([out[j] for j in range(2 * count)], axis=1)


def solution(mesh):
    placed = (
        P("dp", "tensor"),
        P("dp", "tensor"),
        P("dp", "tensor"),
        P("dp"),
        P("dp", "tensor"),
        P(("tensor", "dp"), None),
    )
    return jax.shard_map(
        shards, mesh=mesh, in_specs=placed, out_specs=P("dp", "tensor"), check_vma=False
    )
```

```python
import functools
import math

import jax
import jax.numpy as jnp
from jax import lax
from jax.experimental import pallas as pl
from jax.experimental.pallas import tpu as pltpu
from jax.sharding import PartitionSpec as P

inv_root = 1.0 / math.sqrt(2.0 * math.pi)
sixths = (1, 2, 2, 1)
f32 = jnp.float32
bf16 = jnp.bfloat16


def folded(n):
    return [0] + list(range(1, n, 2)) + list(range(n - 2 + n % 2, 0, -2)) if n > 1 else [0]


def shift(n, stride, total, by):
    pairs = []
    for i in range(total):
        digit = (i // stride) % n
        pairs.append((i, i + (((digit + by) % n) - digit) * stride))
    return pairs


light = pl.CostEstimate(flops=0, bytes_accessed=1024, transcendentals=0)


def params(mib):
    return pltpu.CompilerParams(vmem_limit_bytes=mib * 1024 * 1024)


def split_body(count, half, core, at, *refs):
    pieces = refs[:count]
    outs, held, sems = refs[-4:-2], refs[-2], refs[-1]
    copies = []
    for i in range(count):
        rows = pl.ds(pl.multiple_of(at[i] * half, half), half)
        for k, which in enumerate((core[0], 1 - core[0])):
            slot = 2 * i + k
            cols = pl.ds(pl.multiple_of(which * half, 128), half)
            held[slot] = pieces[i][:, cols].T
            copies.append(pltpu.make_async_copy(held.at[slot], outs[k].at[rows], sems.at[slot]))
            copies[-1].start()
    for c in copies:
        c.wait()


def split_cores(pieces, at, core, slots, before=()):
    count = len(pieces)
    tok, wide = pieces[0].shape
    half = wide // 2
    shape = jax.ShapeDtypeStruct((slots * half, tok), bf16)
    return pl.pallas_call(
        functools.partial(split_body, count, half),
        grid_spec=pltpu.PrefetchScalarGridSpec(
            num_scalar_prefetch=2,
            grid=(1,),
            in_specs=[whole((tok, wide))] * count
            + [pl.BlockSpec(memory_space=pl.ANY)] * len(before),
            out_specs=[pl.BlockSpec(memory_space=pl.ANY)] * 2,
            scratch_shapes=[
                pltpu.VMEM((2 * count, half, tok), bf16),
                pltpu.SemaphoreType.DMA((2 * count,)),
            ],
        ),
        out_shape=[shape, shape],
        input_output_aliases={2 + count: 0, 3 + count: 1} if before else {},
        compiler_params=params(16),
        cost_estimate=light,
        name="split_cores",
    )(core.reshape(1), at, *pieces, *before)


def split_plain(pieces, at, core):
    tok, wide = pieces[0].shape
    full = jnp.zeros((tok, wide * len(pieces)), pieces[0].dtype)
    for i, piece in enumerate(pieces):
        full = lax.dynamic_update_slice(full, piece, (0, at[i] * wide))
    full = full.reshape(tok, len(pieces), 2, wide // 2)
    return [
        lax.dynamic_index_in_dim(full, which, 2, keepdims=False).reshape(tok, -1).T
        for which in (core, 1 - core)
    ]


def whole(shape):
    return pl.BlockSpec(
        shape, lambda *_: (0,) * len(shape), pipeline_mode=pl.Buffered(buffer_count=1)
    )


def bent_body(count, parts, width, at, scale, codes, down, *refs):
    shards, out = refs[: count * parts], refs[count * parts]
    for h in range(parts):
        tall = shards[h].shape[0]
        total = None
        for s in range(count):
            cols = pl.ds(pl.multiple_of(at[s] * width, 128), width)
            term = lax.dot_general(
                shards[s * parts + h][...],
                down[:, cols],
                (((1,), (1,)), ((), ())),
                preferred_element_type=f32,
            )
            total = term if total is None else total + term
        rows = pl.ds(h * tall, tall)
        active = codes[rows, :].astype(f32) * scale[rows, :]
        square = active * active
        out[rows, :] = total * (jnp.exp(-0.5 * square) * inv_root * (2.0 - square))


def bent_of(shards, at, row_scale, codes, down_full):
    count, parts = len(shards), len(shards[0])
    tall, width = shards[0][0].shape
    tok = tall * parts
    wide, feats = down_full.shape
    tile = math.gcd(wide, 512)
    return pl.pallas_call(
        functools.partial(bent_body, count, parts, width),
        grid_spec=pltpu.PrefetchScalarGridSpec(
            num_scalar_prefetch=1,
            grid=(wide // tile,),
            in_specs=[
                whole((tok, 1)),
                pl.BlockSpec((tok, tile), lambda j, at: (0, j)),
                pl.BlockSpec((tile, feats), lambda j, at: (j, 0)),
            ]
            + [whole((tall, width))] * (count * parts),
            out_specs=pl.BlockSpec((tok, tile), lambda j, at: (0, j)),
        ),
        out_shape=jax.ShapeDtypeStruct((tok, wide), f32),
        compiler_params=params(32),
        cost_estimate=light,
        name="bent",
    )(at, row_scale[:, None], codes, down_full, *[p for piece in shards for p in piece])


def partial_body(count, parts, width, spots, plan, arrays, tile, at, slots, *refs):
    pieces, refs = refs[:arrays], refs[arrays:]
    shards = refs[: count * parts]
    out, last, held, sems = refs[count * parts :]
    step = pl.program_id(0)

    @pl.when(step == 0)
    def _():
        copies = []
        for i, (which, first, size) in enumerate(plan):
            into = held.at[pl.ds(pl.multiple_of(slots[i] * spots, spots), size)]
            source = pieces[which].at[pl.ds(first, size)]
            copies.append(pltpu.make_async_copy(source, into, sems.at[i]))
        for c in copies:
            c.start()
        for c in copies:
            c.wait()

    cols = pl.ds(pl.multiple_of(step * tile, tile), tile)
    for h in range(parts):
        tall = shards[h].shape[0]
        total = None
        for s in range(count):
            rows = pl.ds(pl.multiple_of(at[s] * width, width), width)
            term = jnp.dot(
                shards[s * parts + h][...], held[rows, cols], preferred_element_type=f32
            )
            total = term if total is None else total + term
        out[pl.ds(h * tall, tall), :] = total
    last[...] = held[pl.ds(pl.multiple_of(at[count] * width, width), width), cols]


def partial_tangent(shards, at, pieces, slots, spots, feats):
    count, parts = len(shards), len(shards[0])
    tall, width = shards[0][0].shape
    tok = tall * parts
    hidden = pieces[0][0].shape[1]
    tile = 512
    arrays, plan = [], []
    for piece, first, size in pieces:
        which = [i for i, a in enumerate(arrays) if a is piece]
        if not which:
            arrays.append(piece)
        plan.append((which[0] if which else len(arrays) - 1, first, size))
    return pl.pallas_call(
        functools.partial(
            partial_body, count, parts, width, spots, plan, len(arrays), tile
        ),
        grid_spec=pltpu.PrefetchScalarGridSpec(
            num_scalar_prefetch=2,
            grid=(hidden // tile,),
            in_specs=[pl.BlockSpec(memory_space=pl.ANY)] * len(arrays)
            + [whole((tall, width))] * (count * parts),
            out_specs=[
                pl.BlockSpec((tok, tile), lambda j, *_: (0, j)),
                pl.BlockSpec((width, tile), lambda j, *_: (0, j)),
            ],
            scratch_shapes=[
                pltpu.VMEM((feats, hidden), bf16),
                pltpu.SemaphoreType.DMA((len(pieces),)),
            ],
        ),
        out_shape=[
            jax.ShapeDtypeStruct((tok, hidden), f32),
            jax.ShapeDtypeStruct((width, hidden), bf16),
        ],
        compiler_params=params(36),
        cost_estimate=light,
        name="partial_tangent",
    )(at, slots, *arrays, *[p for piece in shards for p in piece])


def front_body(shard, probe, begun, bent, other, mixed, away):
    tangent = begun[...] + jnp.dot(shard[...], probe[...], preferred_element_type=f32)
    mixed[...] = (bent[...] * tangent).astype(bf16)
    away[...] = jnp.dot(other[...], mixed[...], preferred_element_type=f32).astype(bf16)


def front_of(shard, last, begun, bent, other, first, wide):
    tok, width = shard.shape
    half = other.shape[0]
    tile = math.gcd(wide, math.gcd(first, 256))
    base = first // tile
    return pl.pallas_call(
        front_body,
        grid=(wide // tile,),
        in_specs=[
            whole((tok, width)),
            pl.BlockSpec((width, tile), lambda j: (0, base + j)),
            pl.BlockSpec((tok, tile), lambda j: (0, base + j)),
            pl.BlockSpec((tok, tile), lambda j: (0, base + j)),
            whole(other.shape),
        ],
        out_specs=[
            pl.BlockSpec((tok, tile), lambda j: (0, j)),
            pl.BlockSpec((half, tile), lambda j: (0, j)),
        ],
        out_shape=[
            jax.ShapeDtypeStruct((tok, wide), bf16),
            jax.ShapeDtypeStruct((half, wide), bf16),
        ],
        compiler_params=params(20),
        cost_estimate=light,
        name="front",
    )(shard, last, begun, bent, other)


def back_body(xs, ys, rows, steps, me, mine, mixed, came, keep_x, keep_y, to_x, to_y):
    x, y = me[0], me[1]

    def block(at_y, at_x):
        part = pl.ds(pl.multiple_of((at_y * xs + at_x) * rows, rows), rows)
        total = jnp.dot(mine[part, :], mixed[...], preferred_element_type=f32)
        return total + came[part, :].astype(f32)

    @pl.when(pl.program_id(0) < steps)
    def _():
        for k in range(ys):
            for i in range(1, xs):
                to_x[k, i - 1] = block(k, lax.rem(x + i, xs)).astype(bf16)
            keep_x[k, 0] = block(k, x)

    @pl.when(pl.program_id(0) >= steps)
    def _():
        for i in range(xs):
            for k in range(1, ys):
                to_y[k - 1, i] = block(lax.rem(y + k, ys), i).astype(bf16)
            keep_y[0, i] = block(y, i)


def back_of(mine, mixed, came, x, y, xs, ys, rows):
    tok, wide = mixed.shape
    side = wide // 2
    tile = math.gcd(side, 256)
    steps = side // tile

    def left(j, me):
        return (0, 0, 0, jnp.minimum(j, steps - 1))

    def right(j, me):
        return (0, 0, 0, jnp.maximum(j - steps, 0))

    shapes = [(ys, 1, rows), (1, xs, rows), (ys, xs - 1, rows), (ys - 1, xs, rows)]
    kinds = [f32, f32, bf16, bf16]
    return pl.pallas_call(
        functools.partial(back_body, xs, ys, rows, steps),
        grid_spec=pltpu.PrefetchScalarGridSpec(
            num_scalar_prefetch=1,
            grid=(2 * steps,),
            in_specs=[
                whole(mine.shape),
                pl.BlockSpec((tok, tile), lambda j, me: (0, j)),
                pl.BlockSpec((mine.shape[0], tile), lambda j, me: (0, j)),
            ],
            out_specs=[
                pl.BlockSpec(shape + (tile,), where)
                for shape, where in zip(shapes, (left, right, left, right))
            ],
        ),
        out_shape=[
            jax.ShapeDtypeStruct(shape + (side,), kind) for shape, kind in zip(shapes, kinds)
        ],
        compiler_params=params(18),
        cost_estimate=light,
        name="back",
    )(jnp.stack([x, y]), mine, mixed, came)


def after(ready, *values):
    out = lax.optimization_barrier((ready, *values))
    return out[0], (out[1] if len(values) == 1 else list(out[1:]))


def ring_step(block, order):
    n = len(order)
    pairs = [(order[i], order[(i + 1) % n]) for i in range(n)]
    return lax.ppermute(block, "tensor", pairs)


def swapped(block, dp, cores):
    return lax.ppermute(block, "dp", shift(cores, 1, dp, 1))


def parted(parts, dim, n, digit):
    own = lax.dynamic_index_in_dim(parts, digit, dim, keepdims=True)
    sends = [
        lax.dynamic_index_in_dim(parts, lax.rem(digit + by, n), dim, keepdims=True).astype(bf16)
        for by in range(1, n)
    ]
    return own, sends


def sent(sends, n, stride, total):
    return [
        lax.ppermute(send, "dp", shift(n, stride, total, by + 1)) for by, send in enumerate(sends)
    ]


def summed(own, received):
    for r in received:
        own = own + r.astype(f32)
    return own


def shards(tokens, cotangent, codes, row_scale, probe, down_weight):
    dp, tp = lax.axis_size("dp"), lax.axis_size("tensor")
    cores, xs = 2, 2
    ys = dp // (cores * xs)
    me = lax.axis_index("dp")
    core, x, y = lax.rem(me, cores), lax.rem(lax.div(me, cores), xs), lax.div(me, cores * xs)
    tok_rows = tokens.shape[0]
    rows, hidden = probe.shape
    order = folded(tp)
    table = [[order[(order.index(i) - s) % tp] for s in range(tp)] for i in range(tp)]
    at = lax.dynamic_index_in_dim(
        jnp.array(table, jnp.int32), lax.axis_index("tensor"), 0, keepdims=False
    )

    edges = [hidden * sum(sixths[:j]) // sum(sixths) for j in range(len(sixths) + 1)]
    x_way, y_way = (xs, cores), (ys, cores * xs)

    def over(block, way, by):
        return lax.ppermute(block, "dp", shift(way[0], way[1], dp, by))

    cot, tok = [cotangent], [tokens]
    for s in range(1, tp):
        cot.append(ring_step(cot[-1], order))
        tok.append(ring_step(tok[-1], order))
        if s == 1:
            across = [over(probe, x_way, i) for i in range(1, xs)]
            above = [over(probe, y_way, k) for k in range(1, ys)]
            far = []
            for i in range(1, xs):
                for k in range(1, ys):
                    far.append(over(across[i - 1][: rows // 2], y_way, k))
                    far.append(over(above[k - 1][rows // 2 :], x_way, i))
            near = [(p, swapped(p, dp, cores)) for p in (probe, *across, *above)]
        if s < tp - 1:
            cot[s], tok[s] = lax.optimization_barrier((cot[s], tok[s]))
    far = [(p, swapped(p, dp, cores)) for p in far]
    down_full = lax.all_gather(down_weight, "dp", axis=0, tiled=True)

    pieces, slots = [], []

    def hold(pair, half, i, k):
        chip = (lax.rem(y + ys - k, ys) * xs + lax.rem(x + xs - i, xs)) * cores
        for piece, whose in zip(pair, (core, 1 - core)):
            pieces.append((piece, 0, piece.shape[0]))
            slots.append((chip + whose) * 2 + half)

    spots = [(0, 0)] + [(i, 0) for i in range(1, xs)] + [(0, k) for k in range(1, ys)]
    for pair, (i, k) in zip(near, spots):
        hold(pair, 0, i, k)
    spots = [(half, i, k) for i in range(1, xs) for k in range(1, ys) for half in range(2)]
    for pair, spot in zip(far, spots):
        hold(pair, *spot)
    begun, last = partial_tangent(
        [[t] for t in tok[:-1]], at, pieces, jnp.stack(slots), rows // 2, rows * dp
    )
    begun, cot[-1] = after(begun, cot[-1])
    plain = rows % 128 != 0
    if not plain:
        early = list(split_cores(tok[:-1], at[:-1], core, tp))
        early[0], cot[-1] = after(early[0], cot[-1])
    bent = bent_of([[c] for c in cot], at, row_scale, codes, down_full)
    bent, tok[-1] = lax.optimization_barrier((bent, tok[-1]))
    if plain:
        mine, other = split_plain(tok, at, core)
    else:
        mine, other = split_cores(tok[-1:], at[-1:], core, tp, early)

    count = len(sixths)
    out = {}

    def finish(j, keeps, arrived):
        middle = (edges[j] + edges[j + 1]) // 2
        for k, (a, b) in enumerate(((edges[j], middle), (middle, edges[j + 1]))):
            hessian = summed(keeps[k], arrived[k]).reshape(rows, b - a)
            out[2 * j + k] = probe[:, a:b].astype(f32) * hessian * (1.0 / (tok_rows * dp))

    def front(j, ready):
        return front_of(tok[-1], ready, begun, bent, other, edges[j], edges[j + 1] - edges[j])

    fronts = {0: front(0, last)}
    came = {0: swapped(fronts[0][1], dp, cores)}
    mixed = fronts[0][0]
    if count > 1:
        mixed, last = lax.optimization_barrier((mixed, last))
        following, away = front(1, last)
        mixed, following, away, came[0] = lax.optimization_barrier(
            (mixed, following, away, came[0])
        )
        came[1] = swapped(away, dp, cores)
    behind = None
    for j in range(count):
        keep_x, keep_y, to_x, to_y = back_of(mine, mixed, came[j], x, y, xs, ys, rows)
        if behind is not None:
            keeps, arrived = behind
            to_x, to_y, arrived = lax.optimization_barrier((to_x, to_y, arrived))
            finish(j - 1, keeps, arrived)
        ahead = j + 2 < count
        if ahead:
            to_x, to_y, last = lax.optimization_barrier((to_x, to_y, last))
        from_x = [over(to_x[:, i - 1 : i], x_way, i) for i in range(1, xs)]
        from_y = [over(to_y[k - 1 : k], y_way, k) for k in range(1, ys)]
        if ahead:
            beyond, away = front(j + 2, last)
            from_x, from_y, away = lax.optimization_barrier((from_x, from_y, away))
            came[j + 2] = swapped(away, dp, cores)
        left, left_sends = parted(summed(keep_x, from_x), 0, ys, y)
        right, right_sends = parted(summed(keep_y, from_y), 1, xs, x)
        if j + 1 < count:
            left_sends, right_sends, mixed = lax.optimization_barrier(
                (left_sends, right_sends, following)
            )
        if ahead:
            following = beyond
        behind = (left, right), (sent(left_sends, *y_way, dp), sent(right_sends, *x_way, dp))
    finish(count - 1, *behind)
    return jnp.concatenate([out[j] for j in range(2 * count)], axis=1)


def solution(mesh):
    placed = (
        P("dp", "tensor"),
        P("dp", "tensor"),
        P("dp", "tensor"),
        P("dp"),
        P("dp", "tensor"),
        P(("tensor", "dp"), None),
    )
    return jax.shard_map(
        shards, mesh=mesh, in_specs=placed, out_specs=P("dp", "tensor"), check_vma=False
    )
```

```python
import functools
import math

import jax
import jax.numpy as jnp
from jax import lax
from jax.experimental import pallas as pl
from jax.experimental.pallas import tpu as pltpu
from jax.sharding import PartitionSpec as P

inv_root = 1.0 / math.sqrt(2.0 * math.pi)
sixths = (1, 2, 2, 1)
f32 = jnp.float32
bf16 = jnp.bfloat16


def folded(n):
    return [0] + list(range(1, n, 2)) + list(range(n - 2 + n % 2, 0, -2)) if n > 1 else [0]


def shift(n, stride, total, by):
    pairs = []
    for i in range(total):
        digit = (i // stride) % n
        pairs.append((i, i + (((digit + by) % n) - digit) * stride))
    return pairs


light = pl.CostEstimate(flops=0, bytes_accessed=1024, transcendentals=0)


def params(mib):
    return pltpu.CompilerParams(vmem_limit_bytes=mib * 1024 * 1024)


def split_body(count, half, core, at, *refs):
    pieces = refs[:count]
    outs, held, sems = refs[-4:-2], refs[-2], refs[-1]
    copies = []
    for i in range(count):
        rows = pl.ds(pl.multiple_of(at[i] * half, half), half)
        for k, which in enumerate((core[0], 1 - core[0])):
            slot = 2 * i + k
            cols = pl.ds(pl.multiple_of(which * half, 128), half)
            held[slot] = pieces[i][:, cols].T
            copies.append(pltpu.make_async_copy(held.at[slot], outs[k].at[rows], sems.at[slot]))
            copies[-1].start()
    for c in copies:
        c.wait()


def split_cores(pieces, at, core, slots, before=()):
    count = len(pieces)
    tok, wide = pieces[0].shape
    half = wide // 2
    shape = jax.ShapeDtypeStruct((slots * half, tok), bf16)
    return pl.pallas_call(
        functools.partial(split_body, count, half),
        grid_spec=pltpu.PrefetchScalarGridSpec(
            num_scalar_prefetch=2,
            grid=(1,),
            in_specs=[whole((tok, wide))] * count
            + [pl.BlockSpec(memory_space=pl.ANY)] * len(before),
            out_specs=[pl.BlockSpec(memory_space=pl.ANY)] * 2,
            scratch_shapes=[
                pltpu.VMEM((2 * count, half, tok), bf16),
                pltpu.SemaphoreType.DMA((2 * count,)),
            ],
        ),
        out_shape=[shape, shape],
        input_output_aliases={2 + count: 0, 3 + count: 1} if before else {},
        compiler_params=params(52),
        cost_estimate=light,
        name="split_cores",
    )(core.reshape(1), at, *pieces, *before)


def split_plain(pieces, at, core):
    tok, wide = pieces[0].shape
    full = jnp.zeros((tok, wide * len(pieces)), pieces[0].dtype)
    for i, piece in enumerate(pieces):
        full = lax.dynamic_update_slice(full, piece, (0, at[i] * wide))
    full = full.reshape(tok, len(pieces), 2, wide // 2)
    return [
        lax.dynamic_index_in_dim(full, which, 2, keepdims=False).reshape(tok, -1).T
        for which in (core, 1 - core)
    ]


def whole(shape):
    return pl.BlockSpec(
        shape, lambda *_: (0,) * len(shape), pipeline_mode=pl.Buffered(buffer_count=1)
    )


def bent_body(count, parts, width, at, scale, codes, down, *refs):
    shards, out = refs[: count * parts], refs[count * parts]
    for h in range(parts):
        tall = shards[h].shape[0]
        total = None
        for s in range(count):
            cols = pl.ds(pl.multiple_of(at[s] * width, 128), width)
            term = lax.dot_general(
                shards[s * parts + h][...],
                down[:, cols],
                (((1,), (1,)), ((), ())),
                preferred_element_type=f32,
            )
            total = term if total is None else total + term
        rows = pl.ds(h * tall, tall)
        active = codes[rows, :].astype(f32) * scale[rows, :]
        square = active * active
        out[rows, :] = total * (jnp.exp(-0.5 * square) * inv_root * (2.0 - square))


def bent_of(shards, at, scale, codes, down_full, tile):
    count, parts = len(shards), len(shards[0])
    tall, width = shards[0][0].shape
    tok = tall * parts
    wide, feats = down_full.shape
    return pl.pallas_call(
        functools.partial(bent_body, count, parts, width),
        grid_spec=pltpu.PrefetchScalarGridSpec(
            num_scalar_prefetch=1,
            grid=(wide // tile,),
            in_specs=[
                whole((tok, 1)),
                pl.BlockSpec((tok, tile), lambda j, at: (0, j)),
                pl.BlockSpec((tile, feats), lambda j, at: (j, 0)),
            ]
            + [whole((tall, width))] * (count * parts),
            out_specs=pl.BlockSpec((None, tok, tile), lambda j, at: (j, 0, 0)),
        ),
        out_shape=jax.ShapeDtypeStruct((wide // tile, tok, tile), f32),
        compiler_params=params(52),
        cost_estimate=light,
        name="bent",
    )(at, scale, codes, down_full, *[p for piece in shards for p in piece])


def partial_body(count, parts, width, spots, plan, arrays, tile, at, slots, *refs):
    pieces, refs = refs[:arrays], refs[arrays:]
    shards = refs[: count * parts]
    out, last, held, sems = refs[count * parts :]
    step = pl.program_id(0)

    def copies(t):
        cols = pl.ds(t * tile if isinstance(t, int) else pl.multiple_of(t * tile, tile), tile)
        made = []
        for i, (which, first, size) in enumerate(plan):
            into = held.at[pl.ds(pl.multiple_of(slots[i] * spots, spots), size), cols]
            source = pieces[which].at[pl.ds(first, size), cols]
            made.append(pltpu.make_async_copy(source, into, sems.at[t, i]))
        return made

    @pl.when(step == 0)
    def _():
        for t in range(held.shape[1] // tile):
            for c in copies(t):
                c.start()

    for c in copies(step):
        c.wait()

    cols = pl.ds(pl.multiple_of(step * tile, tile), tile)
    for h in range(parts):
        tall = shards[h].shape[0]
        total = None
        for s in range(count):
            rows = pl.ds(pl.multiple_of(at[s] * width, width), width)
            term = jnp.dot(
                shards[s * parts + h][...], held[rows, cols], preferred_element_type=f32
            )
            total = term if total is None else total + term
        out[pl.ds(h * tall, tall), :] = total
    last[...] = held[pl.ds(pl.multiple_of(at[count] * width, width), width), cols]


def partial_tangent(shards, at, pieces, slots, spots, feats, tile):
    count, parts = len(shards), len(shards[0])
    tall, width = shards[0][0].shape
    tok = tall * parts
    hidden = pieces[0][0].shape[1]
    arrays, plan = [], []
    for piece, first, size in pieces:
        which = [i for i, a in enumerate(arrays) if a is piece]
        if not which:
            arrays.append(piece)
        plan.append((which[0] if which else len(arrays) - 1, first, size))
    return pl.pallas_call(
        functools.partial(
            partial_body, count, parts, width, spots, plan, len(arrays), tile
        ),
        grid_spec=pltpu.PrefetchScalarGridSpec(
            num_scalar_prefetch=2,
            grid=(hidden // tile,),
            in_specs=[pl.BlockSpec(memory_space=pl.ANY)] * len(arrays)
            + [whole((tall, width))] * (count * parts),
            out_specs=[
                pl.BlockSpec((None, tok, tile), lambda j, *_: (j, 0, 0)),
                pl.BlockSpec((None, width, tile), lambda j, *_: (j, 0, 0)),
            ],
            scratch_shapes=[
                pltpu.VMEM((feats, hidden), bf16),
                pltpu.SemaphoreType.DMA((hidden // tile, len(pieces))),
            ],
        ),
        out_shape=[
            jax.ShapeDtypeStruct((hidden // tile, tok, tile), f32),
            jax.ShapeDtypeStruct((hidden // tile, width, tile), bf16),
        ],
        compiler_params=params(52),
        cost_estimate=light,
        name="partial_tangent",
    )(at, slots, *arrays, *[p for piece in shards for p in piece])


def front_body(shard, probe, begun, bent, other, mixed, away):
    tangent = begun[...] + jnp.dot(shard[...], probe[...], preferred_element_type=f32)
    mixed[...] = (bent[...] * tangent).astype(bf16)
    away[...] = jnp.dot(other[...], mixed[...], preferred_element_type=f32).astype(bf16)


def front_of(shard, last, begun, bent, other, first, wide):
    tok, width = shard.shape
    half = other.shape[0]
    tile = begun.shape[2]
    base = first // tile
    return pl.pallas_call(
        front_body,
        grid=(wide // tile,),
        in_specs=[
            whole((tok, width)),
            pl.BlockSpec((None, width, tile), lambda j: (base + j, 0, 0)),
            pl.BlockSpec((None, tok, tile), lambda j: (base + j, 0, 0)),
            pl.BlockSpec((None, tok, tile), lambda j: (base + j, 0, 0)),
            whole(other.shape),
        ],
        out_specs=[
            pl.BlockSpec((tok, tile), lambda j: (0, j)),
            pl.BlockSpec((half, tile), lambda j: (0, j)),
        ],
        out_shape=[
            jax.ShapeDtypeStruct((tok, wide), bf16),
            jax.ShapeDtypeStruct((half, wide), bf16),
        ],
        compiler_params=params(52),
        cost_estimate=light,
        name="front",
    )(shard, last, begun, bent, other)


def back_body(xs, ys, rows, steps, me, mine, mixed, came, keep_x, keep_y, to_x, to_y):
    x, y = me[0], me[1]

    def block(at_y, at_x):
        part = pl.ds(pl.multiple_of((at_y * xs + at_x) * rows, rows), rows)
        total = jnp.dot(mine[part, :], mixed[...], preferred_element_type=f32)
        return total + came[part, :].astype(f32)

    @pl.when(pl.program_id(0) < steps)
    def _():
        for k in range(ys):
            for i in range(1, xs):
                to_x[k, i - 1] = block(k, lax.rem(x + i, xs)).astype(bf16)
            keep_x[k, 0] = block(k, x)

    @pl.when(pl.program_id(0) >= steps)
    def _():
        for i in range(xs):
            for k in range(1, ys):
                to_y[k - 1, i] = block(lax.rem(y + k, ys), i).astype(bf16)
            keep_y[0, i] = block(y, i)


def back_of(mine, mixed, came, x, y, xs, ys, rows):
    tok, wide = mixed.shape
    side = wide // 2
    tile = math.gcd(side, 512)
    steps = side // tile

    def left(j, me):
        return (0, 0, 0, jnp.minimum(j, steps - 1))

    def right(j, me):
        return (0, 0, 0, jnp.maximum(j - steps, 0))

    shapes = [(ys, 1, rows), (1, xs, rows), (ys, xs - 1, rows), (ys - 1, xs, rows)]
    kinds = [f32, f32, bf16, bf16]
    return pl.pallas_call(
        functools.partial(back_body, xs, ys, rows, steps),
        grid_spec=pltpu.PrefetchScalarGridSpec(
            num_scalar_prefetch=1,
            grid=(2 * steps,),
            in_specs=[
                whole(mine.shape),
                pl.BlockSpec((tok, tile), lambda j, me: (0, j)),
                pl.BlockSpec((mine.shape[0], tile), lambda j, me: (0, j)),
            ],
            out_specs=[
                pl.BlockSpec(shape + (tile,), where)
                for shape, where in zip(shapes, (left, right, left, right))
            ],
        ),
        out_shape=[
            jax.ShapeDtypeStruct(shape + (side,), kind) for shape, kind in zip(shapes, kinds)
        ],
        compiler_params=params(52),
        cost_estimate=light,
        name="back",
    )(jnp.stack([x, y]), mine, mixed, came)


def after(ready, *values):
    out = lax.optimization_barrier((ready, *values))
    return out[0], (out[1] if len(values) == 1 else list(out[1:]))


def ring_step(block, order):
    n = len(order)
    pairs = [(order[i], order[(i + 1) % n]) for i in range(n)]
    return lax.ppermute(block, "tensor", pairs)


def swapped(block, dp, cores):
    return lax.ppermute(block, "dp", shift(cores, 1, dp, 1))


def parted(parts, dim, n, digit):
    own = lax.dynamic_index_in_dim(parts, digit, dim, keepdims=True)
    sends = [
        lax.dynamic_index_in_dim(parts, lax.rem(digit + by, n), dim, keepdims=True).astype(bf16)
        for by in range(1, n)
    ]
    return own, sends


def sent(sends, n, stride, total):
    return [
        lax.ppermute(send, "dp", shift(n, stride, total, by + 1)) for by, send in enumerate(sends)
    ]


def summed(own, received):
    for r in received:
        own = own + r.astype(f32)
    return own


def shards(tokens, cotangent, codes, row_scale, probe, down_weight):
    dp, tp = lax.axis_size("dp"), lax.axis_size("tensor")
    cores, xs = 2, 2
    ys = dp // (cores * xs)
    me = lax.axis_index("dp")
    core, x, y = lax.rem(me, cores), lax.rem(lax.div(me, cores), xs), lax.div(me, cores * xs)
    tok_rows = tokens.shape[0]
    rows, hidden = probe.shape
    order = folded(tp)
    table = [[order[(order.index(i) - s) % tp] for s in range(tp)] for i in range(tp)]
    at = lax.dynamic_index_in_dim(
        jnp.array(table, jnp.int32), lax.axis_index("tensor"), 0, keepdims=False
    )

    edges = [hidden * sum(sixths[:j]) // sum(sixths) for j in range(len(sixths) + 1)]
    unit = hidden // sum(sixths)
    x_way, y_way = (xs, cores), (ys, cores * xs)
    spots = [(0, 0, 0)] + [(0, i, 0) for i in range(1, xs)] + [(0, 0, k) for k in range(1, ys)]
    spots += [(half, i, k) for i in range(1, xs) for k in range(1, ys) for half in range(2)]
    slots = []
    for half, i, k in spots:
        chip = (lax.rem(y + ys - k, ys) * xs + lax.rem(x + xs - i, xs)) * cores
        slots += [(chip + whose) * 2 + half for whose in (core, 1 - core)]
    slots = jnp.stack(slots)

    def over(block, way, by):
        return lax.ppermute(block, "dp", shift(way[0], way[1], dp, by))

    cot, tok = [cotangent], [tokens]
    for s in range(1, tp):
        cot.append(ring_step(cot[-1], order))
        tok.append(ring_step(tok[-1], order))
        if s == 1:
            across = [over(probe, x_way, i) for i in range(1, xs)]
            above = [over(probe, y_way, k) for k in range(1, ys)]
            far = []
            for i in range(1, xs):
                for k in range(1, ys):
                    far.append(over(across[i - 1][: rows // 2], y_way, k))
                    far.append(over(above[k - 1][rows // 2 :], x_way, i))
            near = [(p, swapped(p, dp, cores)) for p in (probe, *across, *above)]
        if s == 1:
            cot[s], tok[s] = lax.optimization_barrier((cot[s], tok[s]))
        if s == 2:
            near_too = [pair[1] for pair in near]
            cot[s], tok[s], near_too, at, scale, slots = lax.optimization_barrier(
                (cot[s], tok[s], near_too, at, row_scale[:, None], slots)
            )
            near = [(pair[0], other) for pair, other in zip(near, near_too)]
    far = [(p, swapped(p, dp, cores)) for p in far]
    down_full = lax.all_gather(down_weight, "dp", axis=0, tiled=True)

    pieces = [(p, 0, p.shape[0]) for pair in near + far for p in pair]
    begun, last = partial_tangent(
        [[t] for t in tok[:-1]], at, pieces, slots, rows // 2, rows * dp, unit
    )
    begun, cot[-1] = after(begun, cot[-1])
    plain = rows % 128 != 0
    if not plain:
        early = list(split_cores(tok[:-1], at[:-1], core, tp))
        early[0], cot[-1] = after(early[0], cot[-1])
    bent = bent_of([[c] for c in cot], at, scale, codes, down_full, unit)
    bent, tok[-1] = lax.optimization_barrier((bent, tok[-1]))
    if plain:
        mine, other = split_plain(tok, at, core)
    else:
        mine, other = split_cores(tok[-1:], at[-1:], core, tp, early)

    count = len(sixths)
    out = {}

    def finish(j, keeps, arrived):
        middle = (edges[j] + edges[j + 1]) // 2
        for k, (a, b) in enumerate(((edges[j], middle), (middle, edges[j + 1]))):
            hessian = summed(keeps[k], arrived[k]).reshape(rows, b - a)
            out[2 * j + k] = probe[:, a:b].astype(f32) * hessian * (1.0 / (tok_rows * dp))

    def front(j, ready):
        return front_of(tok[-1], ready, begun, bent, other, edges[j], edges[j + 1] - edges[j])

    fronts = {0: front(0, last)}
    came = {0: swapped(fronts[0][1], dp, cores)}
    mixed = fronts[0][0]
    if count > 1:
        mixed, last = lax.optimization_barrier((mixed, last))
        following, away = front(1, last)
        mixed, following, away, came[0] = lax.optimization_barrier(
            (mixed, following, away, came[0])
        )
        came[1] = swapped(away, dp, cores)
    behind = None
    for j in range(count):
        keep_x, keep_y, to_x, to_y = back_of(mine, mixed, came[j], x, y, xs, ys, rows)
        if behind is not None:
            keeps, arrived = behind
            to_x, to_y, arrived = lax.optimization_barrier((to_x, to_y, arrived))
            finish(j - 1, keeps, arrived)
        ahead = j + 2 < count
        if ahead:
            to_x, to_y, last = lax.optimization_barrier((to_x, to_y, last))
        from_x = [over(to_x[:, i - 1 : i], x_way, i) for i in range(1, xs)]
        from_y = [over(to_y[k - 1 : k], y_way, k) for k in range(1, ys)]
        if ahead:
            beyond, away = front(j + 2, last)
            from_x, from_y, away = lax.optimization_barrier((from_x, from_y, away))
            came[j + 2] = swapped(away, dp, cores)
        left, left_sends = parted(summed(keep_x, from_x), 0, ys, y)
        right, right_sends = parted(summed(keep_y, from_y), 1, xs, x)
        if j + 1 < count:
            left_sends, right_sends, mixed = lax.optimization_barrier(
                (left_sends, right_sends, following)
            )
        if ahead:
            following = beyond
        behind = (left, right), (sent(left_sends, *y_way, dp), sent(right_sends, *x_way, dp))
    finish(count - 1, *behind)
    return jnp.concatenate([out[j] for j in range(2 * count)], axis=1)


def solution(mesh):
    placed = (
        P("dp", "tensor"),
        P("dp", "tensor"),
        P("dp", "tensor"),
        P("dp"),
        P("dp", "tensor"),
        P(("tensor", "dp"), None),
    )
    return jax.shard_map(
        shards, mesh=mesh, in_specs=placed, out_specs=P("dp", "tensor"), check_vma=False
    )
```

```python
import functools
import math

import jax
import jax.numpy as jnp
from jax import lax
from jax.experimental import pallas as pl
from jax.experimental.pallas import tpu as pltpu
from jax.sharding import PartitionSpec as P

inv_root = 1.0 / math.sqrt(2.0 * math.pi)
sixths = (2, 1, 2, 1)
f32 = jnp.float32
bf16 = jnp.bfloat16


def folded(n):
    return [0] + list(range(1, n, 2)) + list(range(n - 2 + n % 2, 0, -2)) if n > 1 else [0]


def shift(n, stride, total, by):
    pairs = []
    for i in range(total):
        digit = (i // stride) % n
        pairs.append((i, i + (((digit + by) % n) - digit) * stride))
    return pairs


light = pl.CostEstimate(flops=0, bytes_accessed=1024, transcendentals=0)


def params(mib):
    return pltpu.CompilerParams(vmem_limit_bytes=mib * 1024 * 1024)


def split_body(count, half, core, at, *refs):
    pieces = refs[:count]
    outs, held, sems = refs[-4:-2], refs[-2], refs[-1]
    copies = []
    for i in range(count):
        rows = pl.ds(pl.multiple_of(at[i] * half, half), half)
        for k, which in enumerate((core[0], 1 - core[0])):
            slot = 2 * i + k
            cols = pl.ds(pl.multiple_of(which * half, 128), half)
            held[slot] = pieces[i][:, cols].T
            copies.append(pltpu.make_async_copy(held.at[slot], outs[k].at[rows], sems.at[slot]))
            copies[-1].start()
    for c in copies:
        c.wait()


def split_cores(pieces, at, core, slots, before=()):
    count = len(pieces)
    tok, wide = pieces[0].shape
    half = wide // 2
    shape = jax.ShapeDtypeStruct((slots * half, tok), bf16)
    return pl.pallas_call(
        functools.partial(split_body, count, half),
        grid_spec=pltpu.PrefetchScalarGridSpec(
            num_scalar_prefetch=2,
            grid=(1,),
            in_specs=[whole((tok, wide))] * count
            + [pl.BlockSpec(memory_space=pl.ANY)] * len(before),
            out_specs=[pl.BlockSpec(memory_space=pl.ANY)] * 2,
            scratch_shapes=[
                pltpu.VMEM((2 * count, half, tok), bf16),
                pltpu.SemaphoreType.DMA((2 * count,)),
            ],
        ),
        out_shape=[shape, shape],
        input_output_aliases={2 + count: 0, 3 + count: 1} if before else {},
        compiler_params=params(52),
        cost_estimate=light,
        name="split_cores",
    )(core.reshape(1), at, *pieces, *before)


def split_plain(pieces, at, core):
    tok, wide = pieces[0].shape
    full = jnp.zeros((tok, wide * len(pieces)), pieces[0].dtype)
    for i, piece in enumerate(pieces):
        full = lax.dynamic_update_slice(full, piece, (0, at[i] * wide))
    full = full.reshape(tok, len(pieces), 2, wide // 2)
    return [
        lax.dynamic_index_in_dim(full, which, 2, keepdims=False).reshape(tok, -1).T
        for which in (core, 1 - core)
    ]


def whole(shape):
    return pl.BlockSpec(
        shape, lambda *_: (0,) * len(shape), pipeline_mode=pl.Buffered(buffer_count=1)
    )


def bent_body(count, parts, width, at, scale, codes, down, *refs):
    shards, out = refs[: count * parts], refs[count * parts]
    for h in range(parts):
        tall = shards[h].shape[0]
        total = None
        for s in range(count):
            cols = pl.ds(pl.multiple_of(at[s] * width, 128), width)
            term = lax.dot_general(
                shards[s * parts + h][...],
                down[:, cols],
                (((1,), (1,)), ((), ())),
                preferred_element_type=f32,
            )
            total = term if total is None else total + term
        rows = pl.ds(h * tall, tall)
        active = codes[rows, :].astype(f32) * scale[rows, :]
        square = active * active
        out[rows, :] = total * (jnp.exp(-0.5 * square) * inv_root * (2.0 - square))


def bent_of(shards, at, scale, codes, down_full, tile):
    count, parts = len(shards), len(shards[0])
    tall, width = shards[0][0].shape
    tok = tall * parts
    wide, feats = down_full.shape
    return pl.pallas_call(
        functools.partial(bent_body, count, parts, width),
        grid_spec=pltpu.PrefetchScalarGridSpec(
            num_scalar_prefetch=1,
            grid=(wide // tile,),
            in_specs=[
                whole((tok, 1)),
                pl.BlockSpec((tok, tile), lambda j, at: (0, j)),
                pl.BlockSpec((tile, feats), lambda j, at: (j, 0)),
            ]
            + [whole((tall, width))] * (count * parts),
            out_specs=pl.BlockSpec((None, tok, tile), lambda j, at: (j, 0, 0)),
        ),
        out_shape=jax.ShapeDtypeStruct((wide // tile, tok, tile), f32),
        compiler_params=params(52),
        cost_estimate=light,
        name="bent",
    )(at, scale, codes, down_full, *[p for piece in shards for p in piece])


def partial_body(count, parts, width, spots, plan, arrays, tile, at, slots, *refs):
    pieces, refs = refs[:arrays], refs[arrays:]
    shards = refs[: count * parts]
    out, last, held, sems = refs[count * parts :]
    step = pl.program_id(0)

    def copies(t):
        cols = pl.ds(t * tile if isinstance(t, int) else pl.multiple_of(t * tile, tile), tile)
        made = []
        for i, (which, first, size) in enumerate(plan):
            into = held.at[pl.ds(pl.multiple_of(slots[i] * spots, spots), size), cols]
            source = pieces[which].at[pl.ds(first, size), cols]
            made.append(pltpu.make_async_copy(source, into, sems.at[t, i]))
        return made

    @pl.when(step == 0)
    def _():
        for t in range(held.shape[1] // tile):
            for c in copies(t):
                c.start()

    for c in copies(step):
        c.wait()

    cols = pl.ds(pl.multiple_of(step * tile, tile), tile)
    for h in range(parts):
        tall = shards[h].shape[0]
        total = None
        for s in range(count):
            rows = pl.ds(pl.multiple_of(at[s] * width, width), width)
            term = jnp.dot(
                shards[s * parts + h][...], held[rows, cols], preferred_element_type=f32
            )
            total = term if total is None else total + term
        out[pl.ds(h * tall, tall), :] = total
    last[...] = held[pl.ds(pl.multiple_of(at[count] * width, width), width), cols]


def partial_tangent(shards, at, pieces, slots, spots, feats, tile):
    count, parts = len(shards), len(shards[0])
    tall, width = shards[0][0].shape
    tok = tall * parts
    hidden = pieces[0][0].shape[1]
    arrays, plan = [], []
    for piece, first, size in pieces:
        which = [i for i, a in enumerate(arrays) if a is piece]
        if not which:
            arrays.append(piece)
        plan.append((which[0] if which else len(arrays) - 1, first, size))
    return pl.pallas_call(
        functools.partial(
            partial_body, count, parts, width, spots, plan, len(arrays), tile
        ),
        grid_spec=pltpu.PrefetchScalarGridSpec(
            num_scalar_prefetch=2,
            grid=(hidden // tile,),
            in_specs=[pl.BlockSpec(memory_space=pl.ANY)] * len(arrays)
            + [whole((tall, width))] * (count * parts),
            out_specs=[
                pl.BlockSpec((None, tok, tile), lambda j, *_: (j, 0, 0)),
                pl.BlockSpec((None, width, tile), lambda j, *_: (j, 0, 0)),
            ],
            scratch_shapes=[
                pltpu.VMEM((feats, hidden), bf16),
                pltpu.SemaphoreType.DMA((hidden // tile, len(pieces))),
            ],
        ),
        out_shape=[
            jax.ShapeDtypeStruct((hidden // tile, tok, tile), f32),
            jax.ShapeDtypeStruct((hidden // tile, width, tile), bf16),
        ],
        compiler_params=params(52),
        cost_estimate=light,
        name="partial_tangent",
    )(at, slots, *arrays, *[p for piece in shards for p in piece])


def front_body(shard, probe, begun, bent, other, mixed, away):
    tangent = begun[...] + jnp.dot(shard[...], probe[...], preferred_element_type=f32)
    mixed[...] = (bent[...] * tangent).astype(bf16)
    away[...] = jnp.dot(other[...], mixed[...], preferred_element_type=f32).astype(bf16)


def front_of(shard, last, begun, bent, other, first, wide):
    tok, width = shard.shape
    half = other.shape[0]
    tile = begun.shape[2]
    base = first // tile
    return pl.pallas_call(
        front_body,
        grid=(wide // tile,),
        in_specs=[
            whole((tok, width)),
            pl.BlockSpec((None, width, tile), lambda j: (base + j, 0, 0)),
            pl.BlockSpec((None, tok, tile), lambda j: (base + j, 0, 0)),
            pl.BlockSpec((None, tok, tile), lambda j: (base + j, 0, 0)),
            whole(other.shape),
        ],
        out_specs=[
            pl.BlockSpec((tok, tile), lambda j: (0, j)),
            pl.BlockSpec((half, tile), lambda j: (0, j)),
        ],
        out_shape=[
            jax.ShapeDtypeStruct((tok, wide), bf16),
            jax.ShapeDtypeStruct((half, wide), bf16),
        ],
        compiler_params=params(52),
        cost_estimate=light,
        name="front",
    )(shard, last, begun, bent, other)


def back_body(xs, ys, rows, steps, me, mine, mixed, came, keep_x, keep_y, to_x, to_y):
    x, y = me[0], me[1]

    def block(at_y, at_x):
        part = pl.ds(pl.multiple_of((at_y * xs + at_x) * rows, rows), rows)
        total = jnp.dot(mine[part, :], mixed[...], preferred_element_type=f32)
        return total + came[part, :].astype(f32)

    @pl.when(pl.program_id(0) < steps)
    def _():
        for k in range(ys):
            for i in range(1, xs):
                to_x[k, i - 1] = block(k, lax.rem(x + i, xs)).astype(bf16)
            keep_x[k, 0] = block(k, x)

    @pl.when(pl.program_id(0) >= steps)
    def _():
        for i in range(xs):
            for k in range(1, ys):
                to_y[k - 1, i] = block(lax.rem(y + k, ys), i).astype(bf16)
            keep_y[0, i] = block(y, i)


def back_of(mine, mixed, came, x, y, xs, ys, rows):
    tok, wide = mixed.shape
    side = wide // 2
    tile = math.gcd(side, 512)
    steps = side // tile

    def left(j, me):
        return (0, 0, 0, jnp.minimum(j, steps - 1))

    def right(j, me):
        return (0, 0, 0, jnp.maximum(j - steps, 0))

    shapes = [(ys, 1, rows), (1, xs, rows), (ys, xs - 1, rows), (ys - 1, xs, rows)]
    kinds = [f32, f32, bf16, bf16]
    return pl.pallas_call(
        functools.partial(back_body, xs, ys, rows, steps),
        grid_spec=pltpu.PrefetchScalarGridSpec(
            num_scalar_prefetch=1,
            grid=(2 * steps,),
            in_specs=[
                whole(mine.shape),
                pl.BlockSpec((tok, tile), lambda j, me: (0, j)),
                pl.BlockSpec((mine.shape[0], tile), lambda j, me: (0, j)),
            ],
            out_specs=[
                pl.BlockSpec(shape + (tile,), where)
                for shape, where in zip(shapes, (left, right, left, right))
            ],
        ),
        out_shape=[
            jax.ShapeDtypeStruct(shape + (side,), kind) for shape, kind in zip(shapes, kinds)
        ],
        compiler_params=params(52),
        cost_estimate=light,
        name="back",
    )(jnp.stack([x, y]), mine, mixed, came)


def after(ready, *values):
    out = lax.optimization_barrier((ready, *values))
    return out[0], (out[1] if len(values) == 1 else list(out[1:]))


def ring_step(block, order):
    n = len(order)
    pairs = [(order[i], order[(i + 1) % n]) for i in range(n)]
    return lax.ppermute(block, "tensor", pairs)


def swapped(block, dp, cores):
    return lax.ppermute(block, "dp", shift(cores, 1, dp, 1))


def block_sum(own, received, dim, at):
    total = lax.dynamic_index_in_dim(own, at, dim, keepdims=True)
    for r in received:
        total = total + lax.dynamic_index_in_dim(r, at, dim, keepdims=True).astype(f32)
    return total


def shards(tokens, cotangent, codes, row_scale, probe, down_weight):
    dp, tp = lax.axis_size("dp"), lax.axis_size("tensor")
    cores, xs = 2, 2
    ys = dp // (cores * xs)
    me = lax.axis_index("dp")
    core, x, y = lax.rem(me, cores), lax.rem(lax.div(me, cores), xs), lax.div(me, cores * xs)
    tok_rows = tokens.shape[0]
    rows, hidden = probe.shape
    order = folded(tp)
    table = [[order[(order.index(i) - s) % tp] for s in range(tp)] for i in range(tp)]
    at = lax.dynamic_index_in_dim(
        jnp.array(table, jnp.int32), lax.axis_index("tensor"), 0, keepdims=False
    )

    edges = [hidden * sum(sixths[:j]) // sum(sixths) for j in range(len(sixths) + 1)]
    unit = hidden // sum(sixths)
    x_way, y_way = (xs, cores), (ys, cores * xs)
    spots = [(0, 0, 0)] + [(0, i, 0) for i in range(1, xs)] + [(0, 0, k) for k in range(1, ys)]
    spots += [(half, i, k) for i in range(1, xs) for k in range(1, ys) for half in range(2)]
    slots = []
    for half, i, k in spots:
        chip = (lax.rem(y + ys - k, ys) * xs + lax.rem(x + xs - i, xs)) * cores
        slots += [(chip + whose) * 2 + half for whose in (core, 1 - core)]
    slots = jnp.stack(slots)

    def over(block, way, by):
        return lax.ppermute(block, "dp", shift(way[0], way[1], dp, by))

    cot, tok = [cotangent], [tokens]
    for s in range(1, tp):
        cot.append(ring_step(cot[-1], order))
        tok.append(ring_step(tok[-1], order))
        if s == 1:
            across = [over(probe, x_way, i) for i in range(1, xs)]
            above = [over(probe, y_way, k) for k in range(1, ys)]
            far = []
            for i in range(1, xs):
                for k in range(1, ys):
                    far.append(over(across[i - 1][: rows // 2], y_way, k))
                    far.append(over(above[k - 1][rows // 2 :], x_way, i))
            near = [(p, swapped(p, dp, cores)) for p in (probe, *across, *above)]
        if s == 1:
            cot[s], tok[s] = lax.optimization_barrier((cot[s], tok[s]))
        if s == 2:
            near_too = [pair[1] for pair in near]
            cot[s], tok[s], near_too, at, scale, slots = lax.optimization_barrier(
                (cot[s], tok[s], near_too, at, row_scale[:, None], slots)
            )
            near = [(pair[0], other) for pair, other in zip(near, near_too)]
    plain = rows % 128 != 0
    if not plain:
        early = list(split_cores(tok[:-1], at[:-1], core, tp))
        early[0], far[-1] = lax.optimization_barrier((early[0], far[-1]))
    far = [(p, swapped(p, dp, cores)) for p in far]
    down_full = lax.all_gather(down_weight, "dp", axis=0, tiled=True)

    pieces = [(p, 0, p.shape[0]) for pair in near + far for p in pair]
    begun, last = partial_tangent(
        [[t] for t in tok[:-1]], at, pieces, slots, rows // 2, rows * dp, unit
    )
    begun, cot[-1] = after(begun, cot[-1])
    bent = bent_of([[c] for c in cot], at, scale, codes, down_full, unit)
    bent, tok[-1] = lax.optimization_barrier((bent, tok[-1]))
    if plain:
        mine, other = split_plain(tok, at, core)
    else:
        mine, other = split_cores(tok[-1:], at[-1:], core, tp, early)

    count = len(sixths)
    out = {}

    def front(j, ready):
        return front_of(tok[-1], ready, begun, bent, other, edges[j], edges[j + 1] - edges[j])

    def back(j):
        return back_of(mine, mixed.pop(j), came.pop(j), x, y, xs, ys, rows)

    def first_turn(to_x, to_y):
        return (
            [over(to_x[:, i - 1 : i], x_way, i) for i in range(1, xs)],
            [over(to_y[k - 1 : k], y_way, k) for k in range(1, ys)],
        )

    def finish(j, keeps, first, second):
        middle = (edges[j] + edges[j + 1]) // 2
        for n, (a, b) in enumerate(((edges[j], middle), (middle, edges[j + 1]))):
            total = block_sum(keeps[n], first[n], n, (y, x)[n])
            for r in second[n]:
                total = total + r.astype(f32)
            weight = probe[:, a:b].astype(f32)
            out[2 * j + n] = weight * total.reshape(rows, b - a) * (1.0 / (tok_rows * dp))

    mixed, came, keeps = {}, {}, {}
    mixed[0], away = front(0, last)
    came[0] = swapped(away, dp, cores)
    if count > 1:
        mixed[0], last = lax.optimization_barrier((mixed[0], last))
        mixed[1], away = front(1, last)
        mixed[0], away, came[0] = lax.optimization_barrier((mixed[0], away, came[0]))
        came[1] = swapped(away, dp, cores)
    *keeps[0], to_x, to_y = back(0)
    behind = None
    for j in range(count):
        if j + 1 < count:
            to_x, to_y, mixed[j + 1] = lax.optimization_barrier((to_x, to_y, mixed[j + 1]))
        first = first_turn(to_x, to_y)
        if j + 1 < count:
            *keeps[j + 1], to_x, to_y = back(j + 1)
        if j + 2 < count:
            to_x, to_y, last = lax.optimization_barrier((to_x, to_y, last))
            mixed[j + 2], away = front(j + 2, last)
            first, away, to_x, to_y, behind = lax.optimization_barrier(
                (first, away, to_x, to_y, behind)
            )
            came[j + 2] = swapped(away, dp, cores)
        elif j + 1 < count:
            first, to_x, to_y, behind = lax.optimization_barrier((first, to_x, to_y, behind))
        if j >= 1:
            finish(j - 1, *behind)
        sends_y = [
            block_sum(keeps[j][0], first[0], 0, lax.rem(y + k, ys)).astype(bf16)
            for k in range(1, ys)
        ]
        sends_x = [
            block_sum(keeps[j][1], first[1], 1, lax.rem(x + i, xs)).astype(bf16)
            for i in range(1, xs)
        ]
        if j + 1 < count:
            sends_y, sends_x, to_x, to_y = lax.optimization_barrier(
                (sends_y, sends_x, to_x, to_y)
            )
        second = (
            [over(p, y_way, k + 1) for k, p in enumerate(sends_y)],
            [over(p, x_way, i + 1) for i, p in enumerate(sends_x)],
        )
        behind = (keeps.pop(j), first, second)
    finish(count - 1, *behind)
    return jnp.concatenate([out[j] for j in range(2 * count)], axis=1)


def solution(mesh):
    placed = (
        P("dp", "tensor"),
        P("dp", "tensor"),
        P("dp", "tensor"),
        P("dp"),
        P("dp", "tensor"),
        P(("tensor", "dp"), None),
    )
    return jax.shard_map(
        shards, mesh=mesh, in_specs=placed, out_specs=P("dp", "tensor"), check_vma=False
    )
```

```python
import functools
import math

import jax
import jax.numpy as jnp
from jax import lax
from jax.experimental import pallas as pl
from jax.experimental.pallas import tpu as pltpu
from jax.sharding import PartitionSpec as P

inv_root = 1.0 / math.sqrt(2.0 * math.pi)
sixths = (2, 1, 2, 1)
f32 = jnp.float32
bf16 = jnp.bfloat16


def folded(n):
    return [0] + list(range(1, n, 2)) + list(range(n - 2 + n % 2, 0, -2)) if n > 1 else [0]


def shift(n, stride, total, by):
    pairs = []
    for i in range(total):
        digit = (i // stride) % n
        pairs.append((i, i + (((digit + by) % n) - digit) * stride))
    return pairs


light = pl.CostEstimate(flops=0, bytes_accessed=1024, transcendentals=0)


def params(mib):
    return pltpu.CompilerParams(vmem_limit_bytes=mib * 1024 * 1024)


def split_body(count, half, core, at, *refs):
    pieces = refs[:count]
    outs, held, sems = refs[-4:-2], refs[-2], refs[-1]
    copies = []
    for i in range(count):
        rows = pl.ds(pl.multiple_of(at[i] * half, half), half)
        for k, which in enumerate((core[0], 1 - core[0])):
            slot = 2 * i + k
            cols = pl.ds(pl.multiple_of(which * half, 128), half)
            held[slot] = pieces[i][:, cols].T
            copies.append(pltpu.make_async_copy(held.at[slot], outs[k].at[rows], sems.at[slot]))
            copies[-1].start()
    for c in copies:
        c.wait()


def split_cores(pieces, at, core, slots, before=()):
    count = len(pieces)
    tok, wide = pieces[0].shape
    half = wide // 2
    shape = jax.ShapeDtypeStruct((slots * half, tok), bf16)
    return pl.pallas_call(
        functools.partial(split_body, count, half),
        grid_spec=pltpu.PrefetchScalarGridSpec(
            num_scalar_prefetch=2,
            grid=(1,),
            in_specs=[whole((tok, wide))] * count
            + [pl.BlockSpec(memory_space=pl.ANY)] * len(before),
            out_specs=[pl.BlockSpec(memory_space=pl.ANY)] * 2,
            scratch_shapes=[
                pltpu.VMEM((2 * count, half, tok), bf16),
                pltpu.SemaphoreType.DMA((2 * count,)),
            ],
        ),
        out_shape=[shape, shape],
        input_output_aliases={2 + count: 0, 3 + count: 1} if before else {},
        compiler_params=params(52),
        cost_estimate=light,
        name="split_cores",
    )(core.reshape(1), at, *pieces, *before)


def split_plain(pieces, at, core):
    tok, wide = pieces[0].shape
    full = jnp.zeros((tok, wide * len(pieces)), pieces[0].dtype)
    for i, piece in enumerate(pieces):
        full = lax.dynamic_update_slice(full, piece, (0, at[i] * wide))
    full = full.reshape(tok, len(pieces), 2, wide // 2)
    return [
        lax.dynamic_index_in_dim(full, which, 2, keepdims=False).reshape(tok, -1).T
        for which in (core, 1 - core)
    ]


def whole(shape):
    return pl.BlockSpec(
        shape, lambda *_: (0,) * len(shape), pipeline_mode=pl.Buffered(buffer_count=1)
    )


def bent_body(count, parts, width, at, scale, codes, down, *refs):
    shards, out = refs[: count * parts], refs[count * parts]
    for h in range(parts):
        tall = shards[h].shape[0]
        total = None
        for s in range(count):
            cols = pl.ds(pl.multiple_of(at[s] * width, 128), width)
            term = lax.dot_general(
                shards[s * parts + h][...],
                down[:, cols],
                (((1,), (1,)), ((), ())),
                preferred_element_type=f32,
            )
            total = term if total is None else total + term
        rows = pl.ds(h * tall, tall)
        active = codes[rows, :].astype(f32) * scale[rows, :]
        square = active * active
        out[rows, :] = total * (jnp.exp(-0.5 * square) * inv_root * (2.0 - square))


def bent_of(shards, at, scale, codes, down_full, tile):
    count, parts = len(shards), len(shards[0])
    tall, width = shards[0][0].shape
    tok = tall * parts
    wide, feats = down_full.shape
    return pl.pallas_call(
        functools.partial(bent_body, count, parts, width),
        grid_spec=pltpu.PrefetchScalarGridSpec(
            num_scalar_prefetch=1,
            grid=(wide // tile,),
            in_specs=[
                whole((tok, 1)),
                pl.BlockSpec((tok, tile), lambda j, at: (0, j)),
                pl.BlockSpec((tile, feats), lambda j, at: (j, 0)),
            ]
            + [whole((tall, width))] * (count * parts),
            out_specs=pl.BlockSpec((None, tok, tile), lambda j, at: (j, 0, 0)),
        ),
        out_shape=jax.ShapeDtypeStruct((wide // tile, tok, tile), f32),
        compiler_params=params(52),
        cost_estimate=light,
        name="bent",
    )(at, scale, codes, down_full, *[p for piece in shards for p in piece])


def partial_body(count, parts, width, spots, plan, arrays, tile, at, slots, *refs):
    pieces, refs = refs[:arrays], refs[arrays:]
    shards = refs[: count * parts]
    out, last, held, sems = refs[count * parts :]
    step = pl.program_id(0)

    def copies(t):
        cols = pl.ds(t * tile if isinstance(t, int) else pl.multiple_of(t * tile, tile), tile)
        made = []
        for i, (which, first, size) in enumerate(plan):
            into = held.at[pl.ds(pl.multiple_of(slots[i] * spots, spots), size), cols]
            source = pieces[which].at[pl.ds(first, size), cols]
            made.append(pltpu.make_async_copy(source, into, sems.at[t, i]))
        return made

    @pl.when(step == 0)
    def _():
        for t in range(held.shape[1] // tile):
            for c in copies(t):
                c.start()

    for c in copies(step):
        c.wait()

    cols = pl.ds(pl.multiple_of(step * tile, tile), tile)
    for h in range(parts):
        tall = shards[h].shape[0]
        total = None
        for s in range(count):
            rows = pl.ds(pl.multiple_of(at[s] * width, width), width)
            term = jnp.dot(
                shards[s * parts + h][...], held[rows, cols], preferred_element_type=f32
            )
            total = term if total is None else total + term
        out[pl.ds(h * tall, tall), :] = total
    last[...] = held[pl.ds(pl.multiple_of(at[count] * width, width), width), cols]


def partial_tangent(shards, at, pieces, slots, spots, feats, tile):
    count, parts = len(shards), len(shards[0])
    tall, width = shards[0][0].shape
    tok = tall * parts
    hidden = pieces[0][0].shape[1]
    arrays, plan = [], []
    for piece, first, size in pieces:
        which = [i for i, a in enumerate(arrays) if a is piece]
        if not which:
            arrays.append(piece)
        plan.append((which[0] if which else len(arrays) - 1, first, size))
    return pl.pallas_call(
        functools.partial(
            partial_body, count, parts, width, spots, plan, len(arrays), tile
        ),
        grid_spec=pltpu.PrefetchScalarGridSpec(
            num_scalar_prefetch=2,
            grid=(hidden // tile,),
            in_specs=[pl.BlockSpec(memory_space=pl.ANY)] * len(arrays)
            + [whole((tall, width))] * (count * parts),
            out_specs=[
                pl.BlockSpec((None, tok, tile), lambda j, *_: (j, 0, 0)),
                pl.BlockSpec((None, width, tile), lambda j, *_: (j, 0, 0)),
            ],
            scratch_shapes=[
                pltpu.VMEM((feats, hidden), bf16),
                pltpu.SemaphoreType.DMA((hidden // tile, len(pieces))),
            ],
        ),
        out_shape=[
            jax.ShapeDtypeStruct((hidden // tile, tok, tile), f32),
            jax.ShapeDtypeStruct((hidden // tile, width, tile), bf16),
        ],
        compiler_params=params(52),
        cost_estimate=light,
        name="partial_tangent",
    )(at, slots, *arrays, *[p for piece in shards for p in piece])


def front_body(shard, probe, begun, bent, source, mixed, away, other, sem):
    copy = pltpu.make_async_copy(source, other, sem)
    starting = pl.program_id(0) == 0

    @pl.when(starting)
    def _():
        copy.start()

    tangent = begun[...] + jnp.dot(shard[...], probe[...], preferred_element_type=f32)
    mixed[...] = (bent[...] * tangent).astype(bf16)

    @pl.when(starting)
    def _():
        copy.wait()

    away[...] = jnp.dot(other[...], mixed[...], preferred_element_type=f32).astype(bf16)


def front_of(shard, last, begun, bent, other, first, wide):
    tok, width = shard.shape
    half = other.shape[0]
    tile = begun.shape[2]
    base = first // tile
    return pl.pallas_call(
        front_body,
        grid=(wide // tile,),
        in_specs=[
            whole((tok, width)),
            pl.BlockSpec((None, width, tile), lambda j: (base + j, 0, 0)),
            pl.BlockSpec((None, tok, tile), lambda j: (base + j, 0, 0)),
            pl.BlockSpec((None, tok, tile), lambda j: (base + j, 0, 0)),
            pl.BlockSpec(memory_space=pl.ANY),
        ],
        out_specs=[
            pl.BlockSpec((tok, tile), lambda j: (0, j)),
            pl.BlockSpec((half, tile), lambda j: (0, j)),
        ],
        scratch_shapes=[pltpu.VMEM(other.shape, bf16), pltpu.SemaphoreType.DMA(())],
        out_shape=[
            jax.ShapeDtypeStruct((tok, wide), bf16),
            jax.ShapeDtypeStruct((half, wide), bf16),
        ],
        compiler_params=params(52),
        cost_estimate=light,
        name="front",
    )(shard, last, begun, bent, other)


def back_body(xs, ys, rows, steps, me, source, mixed, came, *refs):
    keep_x, keep_y, to_x, to_y, mine, sems = refs
    x, y = me[0], me[1]
    order = [(k, lax.rem(x + i, xs)) for k in range(ys) for i in [*range(1, xs), 0]]

    def part(at_y, at_x):
        return pl.ds(pl.multiple_of((at_y * xs + at_x) * rows, rows), rows)

    copies = [
        pltpu.make_async_copy(source.at[part(*at)], mine.at[part(*at)], sems.at[n])
        for n, at in enumerate(order)
    ]
    starting = pl.program_id(0) == 0

    @pl.when(starting)
    def _():
        for c in copies:
            c.start()

    def block(at_y, at_x):
        total = jnp.dot(mine[part(at_y, at_x), :], mixed[...], preferred_element_type=f32)
        return total + came[part(at_y, at_x), :].astype(f32)

    @pl.when(pl.program_id(0) < steps)
    def _():
        for n, at in enumerate(order):

            @pl.when(starting)
            def _():
                copies[n].wait()

            k, i = n // xs, n % xs
            if i < xs - 1:
                to_x[k, i] = block(*at).astype(bf16)
            else:
                keep_x[k, 0] = block(*at)

    @pl.when(pl.program_id(0) >= steps)
    def _():
        for i in range(xs):
            for k in range(1, ys):
                to_y[k - 1, i] = block(lax.rem(y + k, ys), i).astype(bf16)
            keep_y[0, i] = block(y, i)


def back_of(mine, mixed, came, x, y, xs, ys, rows):
    tok, wide = mixed.shape
    side = wide // 2
    tile = math.gcd(side, 512)
    steps = side // tile

    def left(j, me):
        return (0, 0, 0, jnp.minimum(j, steps - 1))

    def right(j, me):
        return (0, 0, 0, jnp.maximum(j - steps, 0))

    shapes = [(ys, 1, rows), (1, xs, rows), (ys, xs - 1, rows), (ys - 1, xs, rows)]
    kinds = [f32, f32, bf16, bf16]
    return pl.pallas_call(
        functools.partial(back_body, xs, ys, rows, steps),
        grid_spec=pltpu.PrefetchScalarGridSpec(
            num_scalar_prefetch=1,
            grid=(2 * steps,),
            in_specs=[
                pl.BlockSpec(memory_space=pl.ANY),
                pl.BlockSpec((tok, tile), lambda j, me: (0, j)),
                pl.BlockSpec((mine.shape[0], tile), lambda j, me: (0, j)),
            ],
            out_specs=[
                pl.BlockSpec(shape + (tile,), where)
                for shape, where in zip(shapes, (left, right, left, right))
            ],
            scratch_shapes=[
                pltpu.VMEM(mine.shape, bf16),
                pltpu.SemaphoreType.DMA((xs * ys,)),
            ],
        ),
        out_shape=[
            jax.ShapeDtypeStruct(shape + (side,), kind) for shape, kind in zip(shapes, kinds)
        ],
        compiler_params=params(52),
        cost_estimate=light,
        name="back",
    )(jnp.stack([x, y]), mine, mixed, came)


def after(ready, *values):
    out = lax.optimization_barrier((ready, *values))
    return out[0], (out[1] if len(values) == 1 else list(out[1:]))


def ring_step(block, order):
    n = len(order)
    pairs = [(order[i], order[(i + 1) % n]) for i in range(n)]
    return lax.ppermute(block, "tensor", pairs)


def swapped(block, dp, cores):
    return lax.ppermute(block, "dp", shift(cores, 1, dp, 1))


def block_sum(own, received, dim, at):
    total = lax.dynamic_index_in_dim(own, at, dim, keepdims=True)
    for r in received:
        total = total + lax.dynamic_index_in_dim(r, at, dim, keepdims=True).astype(f32)
    return total


def shards(tokens, cotangent, codes, row_scale, probe, down_weight):
    dp, tp = lax.axis_size("dp"), lax.axis_size("tensor")
    cores, xs = 2, 2
    ys = dp // (cores * xs)
    me = lax.axis_index("dp")
    core, x, y = lax.rem(me, cores), lax.rem(lax.div(me, cores), xs), lax.div(me, cores * xs)
    tok_rows = tokens.shape[0]
    rows, hidden = probe.shape
    order = folded(tp)
    table = [[order[(order.index(i) - s) % tp] for s in range(tp)] for i in range(tp)]
    at = lax.dynamic_index_in_dim(
        jnp.array(table, jnp.int32), lax.axis_index("tensor"), 0, keepdims=False
    )

    edges = [hidden * sum(sixths[:j]) // sum(sixths) for j in range(len(sixths) + 1)]
    unit = hidden // sum(sixths)
    x_way, y_way = (xs, cores), (ys, cores * xs)
    spots = [(0, 0, 0)] + [(0, i, 0) for i in range(1, xs)] + [(0, 0, k) for k in range(1, ys)]
    spots += [(half, i, k) for i in range(1, xs) for k in range(1, ys) for half in range(2)]
    slots = []
    for half, i, k in spots:
        chip = (lax.rem(y + ys - k, ys) * xs + lax.rem(x + xs - i, xs)) * cores
        slots += [(chip + whose) * 2 + half for whose in (core, 1 - core)]
    slots = jnp.stack(slots)

    def over(block, way, by):
        return lax.ppermute(block, "dp", shift(way[0], way[1], dp, by))

    cot, tok = [cotangent], [tokens]
    for s in range(1, tp):
        cot.append(ring_step(cot[-1], order))
        tok.append(ring_step(tok[-1], order))
        if s == 1:
            across = [over(probe, x_way, i) for i in range(1, xs)]
            above = [over(probe, y_way, k) for k in range(1, ys)]
            far = []
            for i in range(1, xs):
                for k in range(1, ys):
                    far.append(over(across[i - 1][: rows // 2], y_way, k))
                    far.append(over(above[k - 1][rows // 2 :], x_way, i))
            near = [(p, swapped(p, dp, cores)) for p in (probe, *across, *above)]
        if s == 1:
            cot[s], tok[s] = lax.optimization_barrier((cot[s], tok[s]))
        if s == 2:
            near_too = [pair[1] for pair in near]
            cot[s], tok[s], near_too, at, scale, slots = lax.optimization_barrier(
                (cot[s], tok[s], near_too, at, row_scale[:, None], slots)
            )
            near = [(pair[0], other) for pair, other in zip(near, near_too)]
    plain = rows % 128 != 0
    if not plain:
        early = list(split_cores(tok[:-1], at[:-1], core, tp))
        early[0], far[-1] = lax.optimization_barrier((early[0], far[-1]))
    far = [(p, swapped(p, dp, cores)) for p in far]
    down_full = lax.all_gather(down_weight, "dp", axis=0, tiled=True)

    pieces = [(p, 0, p.shape[0]) for pair in near + far for p in pair]
    begun, last = partial_tangent(
        [[t] for t in tok[:-1]], at, pieces, slots, rows // 2, rows * dp, unit
    )
    begun, cot[-1] = after(begun, cot[-1])
    bent = bent_of([[c] for c in cot], at, scale, codes, down_full, unit)
    bent, tok[-1] = lax.optimization_barrier((bent, tok[-1]))
    if plain:
        mine, other = split_plain(tok, at, core)
    else:
        mine, other = split_cores(tok[-1:], at[-1:], core, tp, early)

    count = len(sixths)
    out = {}

    def front(j, ready):
        return front_of(tok[-1], ready, begun, bent, other, edges[j], edges[j + 1] - edges[j])

    def back(j):
        return back_of(mine, mixed.pop(j), came.pop(j), x, y, xs, ys, rows)

    def first_turn(to_x, to_y):
        return (
            [over(to_x[:, i - 1 : i], x_way, i) for i in range(1, xs)],
            [over(to_y[k - 1 : k], y_way, k) for k in range(1, ys)],
        )

    def finish(j, keeps, first, second):
        middle = (edges[j] + edges[j + 1]) // 2
        for n, (a, b) in enumerate(((edges[j], middle), (middle, edges[j + 1]))):
            total = block_sum(keeps[n], first[n], n, (y, x)[n])
            for r in second[n]:
                total = total + r.astype(f32)
            weight = probe[:, a:b].astype(f32)
            out[2 * j + n] = weight * total.reshape(rows, b - a) * (1.0 / (tok_rows * dp))

    mixed, came, keeps = {}, {}, {}
    mixed[0], away = front(0, last)
    came[0] = swapped(away, dp, cores)
    if count > 1:
        mixed[0], last = lax.optimization_barrier((mixed[0], last))
        mixed[1], away = front(1, last)
        mixed[0], away, came[0] = lax.optimization_barrier((mixed[0], away, came[0]))
        came[1] = swapped(away, dp, cores)
    *keeps[0], to_x, to_y = back(0)
    behind = None
    for j in range(count):
        if j + 1 < count:
            to_x, to_y, mixed[j + 1] = lax.optimization_barrier((to_x, to_y, mixed[j + 1]))
        first = first_turn(to_x, to_y)
        if j + 1 < count:
            *keeps[j + 1], to_x, to_y = back(j + 1)
        if j + 2 < count:
            to_x, to_y, last = lax.optimization_barrier((to_x, to_y, last))
            mixed[j + 2], away = front(j + 2, last)
            first, away, to_x, to_y, behind = lax.optimization_barrier(
                (first, away, to_x, to_y, behind)
            )
            came[j + 2] = swapped(away, dp, cores)
        elif j + 1 < count:
            first, to_x, to_y, behind = lax.optimization_barrier((first, to_x, to_y, behind))
        if j >= 1:
            finish(j - 1, *behind)
        sends_y = [
            block_sum(keeps[j][0], first[0], 0, lax.rem(y + k, ys)).astype(bf16)
            for k in range(1, ys)
        ]
        sends_x = [
            block_sum(keeps[j][1], first[1], 1, lax.rem(x + i, xs)).astype(bf16)
            for i in range(1, xs)
        ]
        second = (
            [over(p, y_way, k + 1) for k, p in enumerate(sends_y)],
            [over(p, x_way, i + 1) for i, p in enumerate(sends_x)],
        )
        behind = (keeps.pop(j), first, second)
    finish(count - 1, *behind)
    return jnp.concatenate([out[j] for j in range(2 * count)], axis=1)


def solution(mesh):
    placed = (
        P("dp", "tensor"),
        P("dp", "tensor"),
        P("dp", "tensor"),
        P("dp"),
        P("dp", "tensor"),
        P(("tensor", "dp"), None),
    )
    return jax.shard_map(
        shards, mesh=mesh, in_specs=placed, out_specs=P("dp", "tensor"), check_vma=False
    )
```

```python
import functools
import math

import jax
import jax.numpy as jnp
from jax import lax
from jax.experimental import pallas as pl
from jax.experimental.pallas import tpu as pltpu
from jax.sharding import PartitionSpec as P

inv_root = 1.0 / math.sqrt(2.0 * math.pi)
sixths = (2, 1, 2, 1)
f32 = jnp.float32
bf16 = jnp.bfloat16


def folded(n):
    return [0] + list(range(1, n, 2)) + list(range(n - 2 + n % 2, 0, -2)) if n > 1 else [0]


def shift(n, stride, total, by):
    pairs = []
    for i in range(total):
        digit = (i // stride) % n
        pairs.append((i, i + (((digit + by) % n) - digit) * stride))
    return pairs


light = pl.CostEstimate(flops=0, bytes_accessed=1024, transcendentals=0)


def params(mib):
    return pltpu.CompilerParams(vmem_limit_bytes=mib * 1024 * 1024)


def split_body(count, half, core, at, *refs):
    pieces = refs[:count]
    outs, held, sems = refs[-4:-2], refs[-2], refs[-1]
    copies = []
    for i in range(count):
        rows = pl.ds(pl.multiple_of(at[i] * half, half), half)
        for k, which in enumerate((core[0], 1 - core[0])):
            slot = 2 * i + k
            cols = pl.ds(pl.multiple_of(which * half, 128), half)
            held[slot] = pieces[i][:, cols].T
            copies.append(pltpu.make_async_copy(held.at[slot], outs[k].at[rows], sems.at[slot]))
            copies[-1].start()
    for c in copies:
        c.wait()


def split_cores(pieces, at, core, slots, before=()):
    count = len(pieces)
    tok, wide = pieces[0].shape
    half = wide // 2
    shape = jax.ShapeDtypeStruct((slots * half, tok), bf16)
    return pl.pallas_call(
        functools.partial(split_body, count, half),
        grid_spec=pltpu.PrefetchScalarGridSpec(
            num_scalar_prefetch=2,
            grid=(1,),
            in_specs=[whole((tok, wide))] * count
            + [pl.BlockSpec(memory_space=pl.ANY)] * len(before),
            out_specs=[pl.BlockSpec(memory_space=pl.ANY)] * 2,
            scratch_shapes=[
                pltpu.VMEM((2 * count, half, tok), bf16),
                pltpu.SemaphoreType.DMA((2 * count,)),
            ],
        ),
        out_shape=[shape, shape],
        input_output_aliases={2 + count: 0, 3 + count: 1} if before else {},
        compiler_params=params(52),
        cost_estimate=light,
        name="split_cores",
    )(core.reshape(1), at, *pieces, *before)


def split_plain(pieces, at, core):
    tok, wide = pieces[0].shape
    full = jnp.zeros((tok, wide * len(pieces)), pieces[0].dtype)
    for i, piece in enumerate(pieces):
        full = lax.dynamic_update_slice(full, piece, (0, at[i] * wide))
    full = full.reshape(tok, len(pieces), 2, wide // 2)
    return [
        lax.dynamic_index_in_dim(full, which, 2, keepdims=False).reshape(tok, -1).T
        for which in (core, 1 - core)
    ]


def chunk_specs(shape, tile, edges):
    def spec(lo, hi):
        def where(j, *_):
            return (jnp.clip(j - lo, 0, hi - lo - 1), 0, 0)

        return pl.BlockSpec((None,) + shape + (tile,), where)

    return [spec(lo // tile, hi // tile) for lo, hi in zip(edges, edges[1:])]


def chunk_shapes(shape, tile, edges, kind):
    return [
        jax.ShapeDtypeStruct(((hi - lo) // tile,) + shape + (tile,), kind)
        for lo, hi in zip(edges, edges[1:])
    ]


def chunk_store(step, tile, edges, outs, rows, value):
    for out, lo, hi in zip(outs, edges, edges[1:]):

        @pl.when((step >= lo // tile) & (step < hi // tile))
        def _():
            out[rows, :] = value


def whole(shape):
    return pl.BlockSpec(
        shape, lambda *_: (0,) * len(shape), pipeline_mode=pl.Buffered(buffer_count=1)
    )


def bent_body(count, parts, width, tile, edges, at, scale, codes, down, *refs):
    shards, outs = refs[: count * parts], refs[count * parts :]
    for h in range(parts):
        tall = shards[h].shape[0]
        total = None
        for s in range(count):
            cols = pl.ds(pl.multiple_of(at[s] * width, 128), width)
            term = lax.dot_general(
                shards[s * parts + h][...],
                down[:, cols],
                (((1,), (1,)), ((), ())),
                preferred_element_type=f32,
            )
            total = term if total is None else total + term
        rows = pl.ds(h * tall, tall)
        active = codes[rows, :].astype(f32) * scale[rows, :]
        square = active * active
        value = total * (jnp.exp(-0.5 * square) * inv_root * (2.0 - square))
        chunk_store(pl.program_id(0), tile, edges, outs, rows, value)


def bent_of(shards, at, scale, codes, down_full, tile, edges):
    count, parts = len(shards), len(shards[0])
    tall, width = shards[0][0].shape
    tok = tall * parts
    wide, feats = down_full.shape
    return pl.pallas_call(
        functools.partial(bent_body, count, parts, width, tile, edges),
        grid_spec=pltpu.PrefetchScalarGridSpec(
            num_scalar_prefetch=1,
            grid=(wide // tile,),
            in_specs=[
                whole((tok, 1)),
                pl.BlockSpec((tok, tile), lambda j, at: (0, j)),
                pl.BlockSpec((tile, feats), lambda j, at: (j, 0)),
            ]
            + [whole((tall, width))] * (count * parts),
            out_specs=chunk_specs((tok,), tile, edges),
        ),
        out_shape=chunk_shapes((tok,), tile, edges, f32),
        compiler_params=params(52),
        cost_estimate=light,
        name="bent",
    )(at, scale, codes, down_full, *[p for piece in shards for p in piece])


def partial_body(count, parts, width, spots, plan, arrays, tile, edges, at, slots, *refs):
    pieces, refs = refs[:arrays], refs[arrays:]
    shards = refs[: count * parts]
    *outs, last, held, sems = refs[count * parts :]
    step = pl.program_id(0)

    def copies(t):
        cols = pl.ds(t * tile if isinstance(t, int) else pl.multiple_of(t * tile, tile), tile)
        made = []
        for i, (which, first, size) in enumerate(plan):
            into = held.at[pl.ds(pl.multiple_of(slots[i] * spots, spots), size), cols]
            source = pieces[which].at[pl.ds(first, size), cols]
            made.append(pltpu.make_async_copy(source, into, sems.at[t, i]))
        return made

    @pl.when(step == 0)
    def _():
        for t in range(held.shape[1] // tile):
            for c in copies(t):
                c.start()

    for c in copies(step):
        c.wait()

    cols = pl.ds(pl.multiple_of(step * tile, tile), tile)
    for h in range(parts):
        tall = shards[h].shape[0]
        total = None
        for s in range(count):
            rows = pl.ds(pl.multiple_of(at[s] * width, width), width)
            term = jnp.dot(
                shards[s * parts + h][...], held[rows, cols], preferred_element_type=f32
            )
            total = term if total is None else total + term
        chunk_store(step, tile, edges, outs, pl.ds(h * tall, tall), total)
    last[...] = held[pl.ds(pl.multiple_of(at[count] * width, width), width), cols]


def partial_tangent(shards, at, pieces, slots, spots, feats, tile, edges):
    count, parts = len(shards), len(shards[0])
    tall, width = shards[0][0].shape
    tok = tall * parts
    hidden = pieces[0][0].shape[1]
    arrays, plan = [], []
    for piece, first, size in pieces:
        which = [i for i, a in enumerate(arrays) if a is piece]
        if not which:
            arrays.append(piece)
        plan.append((which[0] if which else len(arrays) - 1, first, size))
    return pl.pallas_call(
        functools.partial(
            partial_body, count, parts, width, spots, plan, len(arrays), tile, edges
        ),
        grid_spec=pltpu.PrefetchScalarGridSpec(
            num_scalar_prefetch=2,
            grid=(hidden // tile,),
            in_specs=[pl.BlockSpec(memory_space=pl.ANY)] * len(arrays)
            + [whole((tall, width))] * (count * parts),
            out_specs=[
                *chunk_specs((tok,), tile, edges),
                pl.BlockSpec((None, width, tile), lambda j, *_: (j, 0, 0)),
            ],
            scratch_shapes=[
                pltpu.VMEM((feats, hidden), bf16),
                pltpu.SemaphoreType.DMA((hidden // tile, len(pieces))),
            ],
        ),
        out_shape=[
            *chunk_shapes((tok,), tile, edges, f32),
            jax.ShapeDtypeStruct((hidden // tile, width, tile), bf16),
        ],
        compiler_params=params(52),
        cost_estimate=light,
        name="partial_tangent",
    )(at, slots, *arrays, *[p for piece in shards for p in piece])


def front_body(shard, probe, begun, bent, other, mixed, away):
    tangent = begun[...] + jnp.dot(shard[...], probe[...], preferred_element_type=f32)
    mixed[...] = (bent[...] * tangent).astype(bf16)
    away[...] = jnp.dot(other[...], mixed[...], preferred_element_type=f32).astype(bf16)


def front_of(shard, last, begun, bent, other, first, wide):
    tok, width = shard.shape
    half = other.shape[0]
    tile = begun.shape[2]
    base = first // tile
    return pl.pallas_call(
        front_body,
        grid=(wide // tile,),
        in_specs=[
            whole((tok, width)),
            pl.BlockSpec((None, width, tile), lambda j: (base + j, 0, 0)),
            pl.BlockSpec((None, tok, tile), lambda j: (j, 0, 0)),
            pl.BlockSpec((None, tok, tile), lambda j: (j, 0, 0)),
            whole(other.shape),
        ],
        out_specs=[
            pl.BlockSpec((tok, tile), lambda j: (0, j)),
            pl.BlockSpec((half, tile), lambda j: (0, j)),
        ],
        out_shape=[
            jax.ShapeDtypeStruct((tok, wide), bf16),
            jax.ShapeDtypeStruct((half, wide), bf16),
        ],
        compiler_params=params(40),
        cost_estimate=light,
        name="front",
    )(shard, last, begun, bent, other)


def back_body(xs, ys, rows, steps, me, mine, mixed, came, keep_x, keep_y, to_x, to_y):
    x, y = me[0], me[1]

    def block(at_y, at_x):
        part = pl.ds(pl.multiple_of((at_y * xs + at_x) * rows, rows), rows)
        total = jnp.dot(mine[part, :], mixed[...], preferred_element_type=f32)
        return total + came[part, :].astype(f32)

    @pl.when(pl.program_id(0) < steps)
    def _():
        for k in range(ys):
            for i in range(1, xs):
                to_x[k, i - 1] = block(k, lax.rem(x + i, xs)).astype(bf16)
            keep_x[k, 0] = block(k, x)

    @pl.when(pl.program_id(0) >= steps)
    def _():
        for i in range(xs):
            for k in range(1, ys):
                to_y[k - 1, i] = block(lax.rem(y + k, ys), i).astype(bf16)
            keep_y[0, i] = block(y, i)


def back_of(mine, mixed, came, x, y, xs, ys, rows):
    tok, wide = mixed.shape
    side = wide // 2
    tile = math.gcd(side, 512)
    steps = side // tile

    def left(j, me):
        return (0, 0, 0, jnp.minimum(j, steps - 1))

    def right(j, me):
        return (0, 0, 0, jnp.maximum(j - steps, 0))

    shapes = [(ys, 1, rows), (1, xs, rows), (ys, xs - 1, rows), (ys - 1, xs, rows)]
    kinds = [f32, f32, bf16, bf16]
    return pl.pallas_call(
        functools.partial(back_body, xs, ys, rows, steps),
        grid_spec=pltpu.PrefetchScalarGridSpec(
            num_scalar_prefetch=1,
            grid=(2 * steps,),
            in_specs=[
                whole(mine.shape),
                pl.BlockSpec((tok, tile), lambda j, me: (0, j)),
                pl.BlockSpec((mine.shape[0], tile), lambda j, me: (0, j)),
            ],
            out_specs=[
                pl.BlockSpec(shape + (tile,), where)
                for shape, where in zip(shapes, (left, right, left, right))
            ],
        ),
        out_shape=[
            jax.ShapeDtypeStruct(shape + (side,), kind) for shape, kind in zip(shapes, kinds)
        ],
        compiler_params=params(30),
        cost_estimate=light,
        name="back",
    )(jnp.stack([x, y]), mine, mixed, came)


def after(ready, *values):
    out = lax.optimization_barrier((ready, *values))
    return out[0], (out[1] if len(values) == 1 else list(out[1:]))


def ring_step(block, order):
    n = len(order)
    pairs = [(order[i], order[(i + 1) % n]) for i in range(n)]
    return lax.ppermute(block, "tensor", pairs)


def swapped(block, dp, cores):
    return lax.ppermute(block, "dp", shift(cores, 1, dp, 1))


def block_sum(own, received, dim, at):
    total = lax.dynamic_index_in_dim(own, at, dim, keepdims=True)
    for r in received:
        total = total + lax.dynamic_index_in_dim(r, at, dim, keepdims=True).astype(f32)
    return total


def shards(tokens, cotangent, codes, row_scale, probe, down_weight):
    dp, tp = lax.axis_size("dp"), lax.axis_size("tensor")
    cores, xs = 2, 2
    ys = dp // (cores * xs)
    me = lax.axis_index("dp")
    core, x, y = lax.rem(me, cores), lax.rem(lax.div(me, cores), xs), lax.div(me, cores * xs)
    tok_rows = tokens.shape[0]
    rows, hidden = probe.shape
    order = folded(tp)
    table = [[order[(order.index(i) - s) % tp] for s in range(tp)] for i in range(tp)]
    at = lax.dynamic_index_in_dim(
        jnp.array(table, jnp.int32), lax.axis_index("tensor"), 0, keepdims=False
    )

    edges = [hidden * sum(sixths[:j]) // sum(sixths) for j in range(len(sixths) + 1)]
    unit = hidden // sum(sixths)
    x_way, y_way = (xs, cores), (ys, cores * xs)
    spots = [(0, 0, 0)] + [(0, i, 0) for i in range(1, xs)] + [(0, 0, k) for k in range(1, ys)]
    spots += [(half, i, k) for i in range(1, xs) for k in range(1, ys) for half in range(2)]
    slots = []
    for half, i, k in spots:
        chip = (lax.rem(y + ys - k, ys) * xs + lax.rem(x + xs - i, xs)) * cores
        slots += [(chip + whose) * 2 + half for whose in (core, 1 - core)]
    slots = jnp.stack(slots)

    def over(block, way, by):
        return lax.ppermute(block, "dp", shift(way[0], way[1], dp, by))

    cot, tok = [cotangent], [tokens]
    for s in range(1, tp):
        cot.append(ring_step(cot[-1], order))
        tok.append(ring_step(tok[-1], order))
        if s == 1:
            across = [over(probe, x_way, i) for i in range(1, xs)]
            above = [over(probe, y_way, k) for k in range(1, ys)]
            far = []
            for i in range(1, xs):
                for k in range(1, ys):
                    far.append(over(across[i - 1][: rows // 2], y_way, k))
                    far.append(over(above[k - 1][rows // 2 :], x_way, i))
            near = [(p, swapped(p, dp, cores)) for p in (probe, *across, *above)]
        if s == 1:
            cot[s], tok[s] = lax.optimization_barrier((cot[s], tok[s]))
        if s == 2:
            near_too = [pair[1] for pair in near]
            cot[s], tok[s], near_too, at, scale, slots = lax.optimization_barrier(
                (cot[s], tok[s], near_too, at, row_scale[:, None], slots)
            )
            near = [(pair[0], other) for pair, other in zip(near, near_too)]
    plain = rows % 128 != 0
    if not plain:
        early = list(split_cores(tok[:-1], at[:-1], core, tp))
        early[0], far[-1] = lax.optimization_barrier((early[0], far[-1]))
    far = [(p, swapped(p, dp, cores)) for p in far]
    down_full = lax.all_gather(down_weight, "dp", axis=0, tiled=True)

    pieces = [(p, 0, p.shape[0]) for pair in near + far for p in pair]
    *begun, last = partial_tangent(
        [[t] for t in tok[:-1]], at, pieces, slots, rows // 2, rows * dp, unit, edges
    )
    begun, cot[-1] = after(begun, cot[-1])
    bent = bent_of([[c] for c in cot], at, scale, codes, down_full, unit, edges)
    bent, tok[-1] = lax.optimization_barrier((bent, tok[-1]))
    if plain:
        mine, other = split_plain(tok, at, core)
    else:
        mine, other = split_cores(tok[-1:], at[-1:], core, tp, early)

    count = len(sixths)
    out = {}

    def front(j, ready):
        return front_of(tok[-1], ready, begun[j], bent[j], other, edges[j], edges[j + 1] - edges[j])

    def back(j):
        return back_of(mine, mixed.pop(j), came.pop(j), x, y, xs, ys, rows)

    def first_turn(to_x, to_y):
        return (
            [over(to_x[:, i - 1 : i], x_way, i) for i in range(1, xs)],
            [over(to_y[k - 1 : k], y_way, k) for k in range(1, ys)],
        )

    def finish(j, keeps, first, second):
        middle = (edges[j] + edges[j + 1]) // 2
        for n, (a, b) in enumerate(((edges[j], middle), (middle, edges[j + 1]))):
            total = block_sum(keeps[n], first[n], n, (y, x)[n])
            for r in second[n]:
                total = total + r.astype(f32)
            weight = probe[:, a:b].astype(f32)
            out[2 * j + n] = weight * total.reshape(rows, b - a) * (1.0 / (tok_rows * dp))

    mixed, came, keeps = {}, {}, {}
    mixed[0], away = front(0, last)
    came[0] = swapped(away, dp, cores)
    if count > 1:
        mixed[0], last = lax.optimization_barrier((mixed[0], last))
        mixed[1], away = front(1, last)
        mixed[0], away, came[0] = lax.optimization_barrier((mixed[0], away, came[0]))
        came[1] = swapped(away, dp, cores)
    *keeps[0], to_x, to_y = back(0)
    behind = None
    for j in range(count):
        if j + 1 < count:
            to_x, to_y, mixed[j + 1] = lax.optimization_barrier((to_x, to_y, mixed[j + 1]))
        first = first_turn(to_x, to_y)
        if j + 1 < count:
            *keeps[j + 1], to_x, to_y = back(j + 1)
        if j + 2 < count:
            to_x, to_y, last = lax.optimization_barrier((to_x, to_y, last))
            mixed[j + 2], away = front(j + 2, last)
            first, away, to_x, to_y, behind = lax.optimization_barrier(
                (first, away, to_x, to_y, behind)
            )
            came[j + 2] = swapped(away, dp, cores)
        elif j + 1 < count:
            first, to_x, to_y, behind = lax.optimization_barrier((first, to_x, to_y, behind))
        if j >= 1:
            finish(j - 1, *behind)
        sends_y = [
            block_sum(keeps[j][0], first[0], 0, lax.rem(y + k, ys)).astype(bf16)
            for k in range(1, ys)
        ]
        sends_x = [
            block_sum(keeps[j][1], first[1], 1, lax.rem(x + i, xs)).astype(bf16)
            for i in range(1, xs)
        ]
        second = (
            [over(p, y_way, k + 1) for k, p in enumerate(sends_y)],
            [over(p, x_way, i + 1) for i, p in enumerate(sends_x)],
        )
        behind = (keeps.pop(j), first, second)
    finish(count - 1, *behind)
    return jnp.concatenate([out[j] for j in range(2 * count)], axis=1)


def solution(mesh):
    placed = (
        P("dp", "tensor"),
        P("dp", "tensor"),
        P("dp", "tensor"),
        P("dp"),
        P("dp", "tensor"),
        P(("tensor", "dp"), None),
    )
    return jax.shard_map(
        shards, mesh=mesh, in_specs=placed, out_specs=P("dp", "tensor"), check_vma=False
    )
```

```python
import functools
import math

import jax
import jax.numpy as jnp
from jax import lax
from jax.experimental import pallas as pl
from jax.experimental.pallas import tpu as pltpu
from jax.sharding import PartitionSpec as P

inv_root = 1.0 / math.sqrt(2.0 * math.pi)
sixths = (2, 1, 2, 1)
f32 = jnp.float32
bf16 = jnp.bfloat16


def folded(n):
    return [0] + list(range(1, n, 2)) + list(range(n - 2 + n % 2, 0, -2)) if n > 1 else [0]


def shift(n, stride, total, by):
    pairs = []
    for i in range(total):
        digit = (i // stride) % n
        pairs.append((i, i + (((digit + by) % n) - digit) * stride))
    return pairs


light = pl.CostEstimate(flops=0, bytes_accessed=1024, transcendentals=0)


def params(mib):
    return pltpu.CompilerParams(vmem_limit_bytes=mib * 1024 * 1024)


def split_body(count, half, core, at, *refs):
    pieces = refs[:count]
    outs, held, sems = refs[-4:-2], refs[-2], refs[-1]
    copies = []
    for i in range(count):
        rows = pl.ds(pl.multiple_of(at[i] * half, half), half)
        for k, which in enumerate((core[0], 1 - core[0])):
            slot = 2 * i + k
            cols = pl.ds(pl.multiple_of(which * half, 128), half)
            held[slot] = pieces[i][:, cols].T
            copies.append(pltpu.make_async_copy(held.at[slot], outs[k].at[rows], sems.at[slot]))
            copies[-1].start()
    for c in copies:
        c.wait()


def split_cores(pieces, at, core, slots, before=()):
    count = len(pieces)
    tok, wide = pieces[0].shape
    half = wide // 2
    shape = jax.ShapeDtypeStruct((slots * half, tok), bf16)
    return pl.pallas_call(
        functools.partial(split_body, count, half),
        grid_spec=pltpu.PrefetchScalarGridSpec(
            num_scalar_prefetch=2,
            grid=(1,),
            in_specs=[whole((tok, wide))] * count
            + [pl.BlockSpec(memory_space=pl.ANY)] * len(before),
            out_specs=[pl.BlockSpec(memory_space=pl.ANY)] * 2,
            scratch_shapes=[
                pltpu.VMEM((2 * count, half, tok), bf16),
                pltpu.SemaphoreType.DMA((2 * count,)),
            ],
        ),
        out_shape=[shape, shape],
        input_output_aliases={2 + count: 0, 3 + count: 1} if before else {},
        compiler_params=params(52),
        cost_estimate=light,
        name="split_cores",
    )(core.reshape(1), at, *pieces, *before)


def split_plain(pieces, at, core):
    tok, wide = pieces[0].shape
    full = jnp.zeros((tok, wide * len(pieces)), pieces[0].dtype)
    for i, piece in enumerate(pieces):
        full = lax.dynamic_update_slice(full, piece, (0, at[i] * wide))
    full = full.reshape(tok, len(pieces), 2, wide // 2)
    return [
        lax.dynamic_index_in_dim(full, which, 2, keepdims=False).reshape(tok, -1).T
        for which in (core, 1 - core)
    ]


def whole(shape):
    return pl.BlockSpec(
        shape, lambda *_: (0,) * len(shape), pipeline_mode=pl.Buffered(buffer_count=1)
    )


def bent_body(count, parts, width, at, scale, codes, down, *refs):
    shards, out = refs[: count * parts], refs[count * parts]
    for h in range(parts):
        tall = shards[h].shape[0]
        total = None
        for s in range(count):
            cols = pl.ds(pl.multiple_of(at[s] * width, 128), width)
            term = lax.dot_general(
                shards[s * parts + h][...],
                down[:, cols],
                (((1,), (1,)), ((), ())),
                preferred_element_type=f32,
            )
            total = term if total is None else total + term
        rows = pl.ds(h * tall, tall)
        active = codes[rows, :].astype(f32) * scale[rows, :]
        square = active * active
        out[rows, :] = total * (jnp.exp(-0.5 * square) * inv_root * (2.0 - square))


def bent_of(shards, at, scale, codes, down_full, tile):
    count, parts = len(shards), len(shards[0])
    tall, width = shards[0][0].shape
    tok = tall * parts
    wide, feats = down_full.shape
    return pl.pallas_call(
        functools.partial(bent_body, count, parts, width),
        grid_spec=pltpu.PrefetchScalarGridSpec(
            num_scalar_prefetch=1,
            grid=(wide // tile,),
            in_specs=[
                whole((tok, 1)),
                pl.BlockSpec((tok, tile), lambda j, at: (0, j)),
                pl.BlockSpec((tile, feats), lambda j, at: (j, 0)),
            ]
            + [whole((tall, width))] * (count * parts),
            out_specs=pl.BlockSpec((None, tok, tile), lambda j, at: (j, 0, 0)),
        ),
        out_shape=jax.ShapeDtypeStruct((wide // tile, tok, tile), f32),
        compiler_params=params(52),
        cost_estimate=light,
        name="bent",
    )(at, scale, codes, down_full, *[p for piece in shards for p in piece])


def partial_body(count, parts, width, spots, plan, arrays, tile, at, slots, *refs):
    pieces, refs = refs[:arrays], refs[arrays:]
    shards = refs[: count * parts]
    out, last, held, sems = refs[count * parts :]
    step = pl.program_id(0)

    def copies(t):
        cols = pl.ds(t * tile if isinstance(t, int) else pl.multiple_of(t * tile, tile), tile)
        made = []
        for i, (which, first, size) in enumerate(plan):
            into = held.at[pl.ds(pl.multiple_of(slots[i] * spots, spots), size), cols]
            source = pieces[which].at[pl.ds(first, size), cols]
            made.append(pltpu.make_async_copy(source, into, sems.at[t, i]))
        return made

    @pl.when(step == 0)
    def _():
        for t in range(held.shape[1] // tile):
            for c in copies(t):
                c.start()

    for c in copies(step):
        c.wait()

    cols = pl.ds(pl.multiple_of(step * tile, tile), tile)
    for h in range(parts):
        tall = shards[h].shape[0]
        total = None
        for s in range(count):
            rows = pl.ds(pl.multiple_of(at[s] * width, width), width)
            term = jnp.dot(
                shards[s * parts + h][...], held[rows, cols], preferred_element_type=f32
            )
            total = term if total is None else total + term
        out[pl.ds(h * tall, tall), :] = total
    last[...] = held[pl.ds(pl.multiple_of(at[count] * width, width), width), cols]


def partial_tangent(shards, at, pieces, slots, spots, feats, tile):
    count, parts = len(shards), len(shards[0])
    tall, width = shards[0][0].shape
    tok = tall * parts
    hidden = pieces[0][0].shape[1]
    arrays, plan = [], []
    for piece, first, size in pieces:
        which = [i for i, a in enumerate(arrays) if a is piece]
        if not which:
            arrays.append(piece)
        plan.append((which[0] if which else len(arrays) - 1, first, size))
    return pl.pallas_call(
        functools.partial(
            partial_body, count, parts, width, spots, plan, len(arrays), tile
        ),
        grid_spec=pltpu.PrefetchScalarGridSpec(
            num_scalar_prefetch=2,
            grid=(hidden // tile,),
            in_specs=[pl.BlockSpec(memory_space=pl.ANY)] * len(arrays)
            + [whole((tall, width))] * (count * parts),
            out_specs=[
                pl.BlockSpec((None, tok, tile), lambda j, *_: (j, 0, 0)),
                pl.BlockSpec((None, width, tile), lambda j, *_: (j, 0, 0)),
            ],
            scratch_shapes=[
                pltpu.VMEM((feats, hidden), bf16),
                pltpu.SemaphoreType.DMA((hidden // tile, len(pieces))),
            ],
        ),
        out_shape=[
            jax.ShapeDtypeStruct((hidden // tile, tok, tile), f32),
            jax.ShapeDtypeStruct((hidden // tile, width, tile), bf16),
        ],
        compiler_params=params(52),
        cost_estimate=light,
        name="partial_tangent",
    )(at, slots, *arrays, *[p for piece in shards for p in piece])


def front_body(shard, probe, begun, bent, other, mixed, away):
    tangent = begun[...] + jnp.dot(shard[...], probe[...], preferred_element_type=f32)
    mixed[...] = (bent[...] * tangent).astype(bf16)
    away[...] = jnp.dot(other[...], mixed[...], preferred_element_type=f32).astype(bf16)


def front_of(shard, last, begun, bent, other, first, wide):
    tok, width = shard.shape
    half = other.shape[0]
    tile = begun.shape[2]
    base = first // tile
    return pl.pallas_call(
        front_body,
        grid=(wide // tile,),
        in_specs=[
            whole((tok, width)),
            pl.BlockSpec((None, width, tile), lambda j: (base + j, 0, 0)),
            pl.BlockSpec((None, tok, tile), lambda j: (base + j, 0, 0)),
            pl.BlockSpec((None, tok, tile), lambda j: (base + j, 0, 0)),
            whole(other.shape),
        ],
        out_specs=[
            pl.BlockSpec((tok, tile), lambda j: (0, j)),
            pl.BlockSpec((half, tile), lambda j: (0, j)),
        ],
        out_shape=[
            jax.ShapeDtypeStruct((tok, wide), bf16),
            jax.ShapeDtypeStruct((half, wide), bf16),
        ],
        compiler_params=params(52),
        cost_estimate=light,
        name="front",
    )(shard, last, begun, bent, other)


def back_body(xs, ys, rows, steps, me, mine, mixed, came, keep_x, keep_y, to_x, to_y):
    x, y = me[0], me[1]

    def block(at_y, at_x):
        part = pl.ds(pl.multiple_of((at_y * xs + at_x) * rows, rows), rows)
        total = jnp.dot(mine[part, :], mixed[...], preferred_element_type=f32)
        return total + came[part, :].astype(f32)

    @pl.when(pl.program_id(0) < steps)
    def _():
        for k in range(ys):
            for i in range(1, xs):
                to_x[k, i - 1] = block(k, lax.rem(x + i, xs)).astype(bf16)
            keep_x[k, 0] = block(k, x)

    @pl.when(pl.program_id(0) >= steps)
    def _():
        for i in range(xs):
            for k in range(1, ys):
                to_y[k - 1, i] = block(lax.rem(y + k, ys), i).astype(bf16)
            keep_y[0, i] = block(y, i)


def back_of(mine, mixed, came, x, y, xs, ys, rows):
    tok, wide = mixed.shape
    side = wide // 2
    tile = math.gcd(side, 512)
    steps = side // tile

    def left(j, me):
        return (0, 0, 0, jnp.minimum(j, steps - 1))

    def right(j, me):
        return (0, 0, 0, jnp.maximum(j - steps, 0))

    shapes = [(ys, 1, rows), (1, xs, rows), (ys, xs - 1, rows), (ys - 1, xs, rows)]
    kinds = [f32, f32, bf16, bf16]
    return pl.pallas_call(
        functools.partial(back_body, xs, ys, rows, steps),
        grid_spec=pltpu.PrefetchScalarGridSpec(
            num_scalar_prefetch=1,
            grid=(2 * steps,),
            in_specs=[
                whole(mine.shape),
                pl.BlockSpec((tok, tile), lambda j, me: (0, j)),
                pl.BlockSpec((mine.shape[0], tile), lambda j, me: (0, j)),
            ],
            out_specs=[
                pl.BlockSpec(shape + (tile,), where)
                for shape, where in zip(shapes, (left, right, left, right))
            ],
        ),
        out_shape=[
            jax.ShapeDtypeStruct(shape + (side,), kind) for shape, kind in zip(shapes, kinds)
        ],
        compiler_params=params(52),
        cost_estimate=light,
        name="back",
    )(jnp.stack([x, y]), mine, mixed, came)


def after(ready, *values):
    out = lax.optimization_barrier((ready, *values))
    return out[0], (out[1] if len(values) == 1 else list(out[1:]))


def ring_step(block, order):
    n = len(order)
    pairs = [(order[i], order[(i + 1) % n]) for i in range(n)]
    return lax.ppermute(block, "tensor", pairs)


def swapped(block, dp, cores):
    return lax.ppermute(block, "dp", shift(cores, 1, dp, 1))


def block_sum(own, received, dim, at):
    total = lax.dynamic_index_in_dim(own, at, dim, keepdims=True)
    for r in received:
        total = total + lax.dynamic_index_in_dim(r, at, dim, keepdims=True).astype(f32)
    return total


def shards(tokens, cotangent, codes, row_scale, probe, down_weight):
    dp, tp = lax.axis_size("dp"), lax.axis_size("tensor")
    cores, xs = 2, 2
    ys = dp // (cores * xs)
    me = lax.axis_index("dp")
    core, x, y = lax.rem(me, cores), lax.rem(lax.div(me, cores), xs), lax.div(me, cores * xs)
    tok_rows = tokens.shape[0]
    rows, hidden = probe.shape
    order = folded(tp)
    table = [[order[(order.index(i) - s) % tp] for s in range(tp)] for i in range(tp)]
    at = lax.dynamic_index_in_dim(
        jnp.array(table, jnp.int32), lax.axis_index("tensor"), 0, keepdims=False
    )

    edges = [hidden * sum(sixths[:j]) // sum(sixths) for j in range(len(sixths) + 1)]
    unit = hidden // sum(sixths)
    x_way, y_way = (xs, cores), (ys, cores * xs)
    spots = [(0, 0, 0)] + [(0, i, 0) for i in range(1, xs)] + [(0, 0, k) for k in range(1, ys)]
    spots += [(half, i, k) for i in range(1, xs) for k in range(1, ys) for half in range(2)]
    slots = []
    for half, i, k in spots:
        chip = (lax.rem(y + ys - k, ys) * xs + lax.rem(x + xs - i, xs)) * cores
        slots += [(chip + whose) * 2 + half for whose in (core, 1 - core)]
    slots = jnp.stack(slots)

    def over(block, way, by):
        return lax.ppermute(block, "dp", shift(way[0], way[1], dp, by))

    cot, tok = [cotangent], [tokens]
    for s in range(1, tp):
        cot.append(ring_step(cot[-1], order))
        tok.append(ring_step(tok[-1], order))
        if s == 1:
            across = [over(probe, x_way, i) for i in range(1, xs)]
            above = [over(probe, y_way, k) for k in range(1, ys)]
            far = []
            for i in range(1, xs):
                for k in range(1, ys):
                    far.append(over(across[i - 1][: rows // 2], y_way, k))
                    far.append(over(above[k - 1][rows // 2 :], x_way, i))
            near = [(p, swapped(p, dp, cores)) for p in (probe, *across, *above)]
        if s == 1:
            cot[s], tok[s] = lax.optimization_barrier((cot[s], tok[s]))
        if s == 2:
            near_too = [pair[1] for pair in near]
            cot[s], tok[s], near_too, at, scale, slots = lax.optimization_barrier(
                (cot[s], tok[s], near_too, at, row_scale[:, None], slots)
            )
            near = [(pair[0], other) for pair, other in zip(near, near_too)]
    plain = rows % 128 != 0
    if not plain:
        early = list(split_cores(tok[:-1], at[:-1], core, tp))
        early[0], far[-1] = lax.optimization_barrier((early[0], far[-1]))
    far = [(p, swapped(p, dp, cores)) for p in far]
    down_full = lax.all_gather(down_weight, "dp", axis=0, tiled=True)

    pieces = [(p, 0, p.shape[0]) for pair in near + far for p in pair]
    begun, last = partial_tangent(
        [[t] for t in tok[:-1]], at, pieces, slots, rows // 2, rows * dp, unit
    )
    begun, cot[-1] = after(begun, cot[-1])
    bent = bent_of([[c] for c in cot], at, scale, codes, down_full, unit)
    bent, tok[-1] = lax.optimization_barrier((bent, tok[-1]))
    if plain:
        mine, other = split_plain(tok, at, core)
    else:
        mine, other = split_cores(tok[-1:], at[-1:], core, tp, early)

    count = len(sixths)
    out = {}

    def front(j, ready):
        return front_of(tok[-1], ready, begun, bent, other, edges[j], edges[j + 1] - edges[j])

    def back(j):
        return back_of(mine, mixed.pop(j), came.pop(j), x, y, xs, ys, rows)

    def first_turn(to_x, to_y):
        return (
            [over(to_x[:, i - 1 : i], x_way, i) for i in range(1, xs)],
            [over(to_y[k - 1 : k], y_way, k) for k in range(1, ys)],
        )

    def finish(j, keeps, first, second):
        middle = (edges[j] + edges[j + 1]) // 2
        for n, (a, b) in enumerate(((edges[j], middle), (middle, edges[j + 1]))):
            total = block_sum(keeps[n], first[n], n, (y, x)[n])
            for r in second[n]:
                total = total + r.astype(f32)
            weight = probe[:, a:b].astype(f32)
            out[2 * j + n] = weight * total.reshape(rows, b - a) * (1.0 / (tok_rows * dp))

    def second_turn(j, first):
        sends_y = [
            block_sum(keeps[j][0], first[0], 0, lax.rem(y + k, ys)).astype(bf16)
            for k in range(1, ys)
        ]
        sends_x = [
            block_sum(keeps[j][1], first[1], 1, lax.rem(x + i, xs)).astype(bf16)
            for i in range(1, xs)
        ]
        return sends_y, sends_x

    def send_second(sends_y, sends_x):
        return (
            [over(p, y_way, k + 1) for k, p in enumerate(sends_y)],
            [over(p, x_way, i + 1) for i, p in enumerate(sends_x)],
        )

    mixed, came, keeps = {}, {}, {}
    mixed[0], away = front(0, last)
    came[0] = swapped(away, dp, cores)
    mixed[0], last = lax.optimization_barrier((mixed[0], last))
    mixed[1], away = front(1, last)
    mixed[0], away, came[0] = lax.optimization_barrier((mixed[0], away, came[0]))
    came[1] = swapped(away, dp, cores)
    *keeps[0], to_x, to_y = back(0)
    waiting = None
    for j in range(0, count, 2):
        more = j + 2 < count
        to_x, to_y, mixed[j + 1] = lax.optimization_barrier((to_x, to_y, mixed[j + 1]))
        first = first_turn(to_x, to_y)
        *keeps[j + 1], next_x, next_y = back(j + 1)
        if more:
            next_x, next_y, last = lax.optimization_barrier((next_x, next_y, last))
        following = first_turn(next_x, next_y)
        if waiting is not None:
            for n, (pair, arrived) in enumerate(waiting):
                finish(j - 2 + n, keeps[j - 2 + n], pair, arrived)
        if more:
            mixed[j + 2], away = front(j + 2, last)
            mixed[j + 3], later = front(j + 3, last)
            first, following, away, later = lax.optimization_barrier(
                (first, following, away, later)
            )
            came[j + 2] = swapped(away, dp, cores)
            came[j + 3] = swapped(later, dp, cores)
        else:
            first, following = lax.optimization_barrier((first, following))
        sends = [second_turn(j, first), second_turn(j + 1, following)]
        if more:
            sends, mixed[j + 2] = lax.optimization_barrier((sends, mixed[j + 2]))
        arrived = [send_second(*pair) for pair in sends]
        if more:
            *keeps[j + 2], to_x, to_y = back(j + 2)
            arrived, to_x, to_y = lax.optimization_barrier((arrived, to_x, to_y))
        waiting = [(first, arrived[0]), (following, arrived[1])]
    for n, (pair, arrived) in enumerate(waiting):
        finish(count - 2 + n, keeps[count - 2 + n], pair, arrived)
    return jnp.concatenate([out[j] for j in range(2 * count)], axis=1)


def solution(mesh):
    placed = (
        P("dp", "tensor"),
        P("dp", "tensor"),
        P("dp", "tensor"),
        P("dp"),
        P("dp", "tensor"),
        P(("tensor", "dp"), None),
    )
    return jax.shard_map(
        shards, mesh=mesh, in_specs=placed, out_specs=P("dp", "tensor"), check_vma=False
    )
```
